128 devices in a mesh: row: 8 (over z, core), col: 16 (over y, x).
Axes of the slice: x: 4, y: 4, z: 4, core: 2. Of those that a mesh axis runs over, the one named last changes fastest.
Arguments:
- operator: float32 [16384, 16384], P('row', 'col'), may hold values from -0.046875 to 0.046875
- vectors: float32 [16384, 256], P('row', 'col'), may hold values from -6 to 6
- owner_map: int32 [11264, 1], P(('row', 'col')), may hold values from 0 to 15; in each aligned block of 88 rows (0 to 87, 88 to 175, ...) at most 16 rows name the same one
- coupling: float32 [8, 512, 1024], P('row', 'col'), may hold values from -0.1875 to 0.1875
- ancestors: int32 [8, 16, 512], P('row', 'col'), may hold values from 0 to 1535, as said below
- leaf_modes: float32 [8, 16, 2048, 256], P('row', 'col'), may hold values from -0.375 to 0.375
- constraint_modes: float32 [8, 16, 2048, 512], P('row', 'col'), may hold values from -0.25 to 0.25
Outputs:
- separators: float32 [8, 512, 256], P('row', 'col')
- interiors: float32 [8, 16, 2048, 256], P('row', 'col')
The draws below stay inside these ranges and needn't reach their ends.
Inputs may be any that keep to these rules, and one draw needn't show every extreme that they name: `owner_map`: in each aligned block of 88 rows no leaf is named more than 16 times, a bound that some block reaches. `ancestors`: the 512 indices of one leaf are distinct.
All inputs are finite; a program needn't handle non-finite values.
Results may differ from the reference program's by a relative error of at most 0.00007.
Values sent between devices are 32-bit elements; how exact they have to be, the bound alone decides.
A program may use at most 64 MiB of HBM per device.

```python
import math
import jax
import jax.numpy as jnp
import numpy as np
from jax import lax

NV = 256
MODES = 256
INTER = 2048
ANC = 512
MODE_DEV = 88
SEP_DEV = 32
ROWS_DEV = 128
SUBS = 8
FANOUT = 16
M = 16384
MOST = 16
OWNED = 11264
TOPU = 1024
SEPU = 512


def draw_ancestors(key, part):
    candidate_total = TOPU + SEPU
    leaf_keys = jax.random.split(key, SUBS * FANOUT)
    selected = jax.vmap(lambda leaf_key: jax.random.permutation(leaf_key, candidate_total)[:ANC])(leaf_keys)
    interior_pick = jax.random.permutation(jax.random.fold_in(key, 7), candidate_total - 2)[:ANC - 2] + 1
    leading = jnp.concatenate([jnp.array([0, candidate_total - 1], jnp.int32), interior_pick.astype(jnp.int32)])
    selected = selected.astype(jnp.int32).at[0].set(leading)
    return selected.reshape(SUBS, FANOUT, ANC)


def shard_levels(stream_key, shape, pieces, low, top_value):
    def one(position, blocks):
        steps = jax.random.uniform(jax.random.fold_in(jax.random.fold_in(stream_key, 6), position), (blocks,), jnp.float32, low / len(pieces), top_value / len(pieces))
        return jnp.repeat(jnp.exp(steps), shape[position] // blocks).reshape((-1,) + (1,) * (len(shape) - position - 1))

    loudness = one(*pieces[0])
    for cut in pieces[1:]:
        loudness = loudness * one(*cut)
    return loudness


def assign_block(rng, own, number, rows, count, top, reach, slope):
    order = jax.random.permutation(rng, count)
    crowded, usual = portions_of(count, rows * top, reach, slope, True), portions_of(count, rows * top, reach, slope, False)
    places = jnp.arange(count)

    def named(sizes, turn):
        used = int((sizes > 0).sum())
        fixed = max(1, used // 4)
        shifted = fixed + (places - fixed + turn * (used - fixed)) % max(1, count - fixed)
        return jnp.zeros((count,), jnp.int32).at[order[jnp.where(places < fixed, places, shifted)]].set(jnp.asarray(sizes, jnp.int32))

    sizes = jnp.where(number % 4 == 0, named(crowded, number // 4), named(usual, number - number // 4 - 1))
    mixed = jax.random.permutation(jax.random.fold_in(own, 3), count)
    donor, receiver = mixed[0:count // 2 * 2:2], mixed[1:count // 2 * 2:2]
    margin = jnp.minimum(sizes[donor] - 1, reach - sizes[receiver]) // 2
    margin = jnp.where((donor == order[0]) | (receiver == order[0]) | (sizes[receiver] == 0), 0, jnp.maximum(margin, 0))
    shifted = jax.random.randint(jax.random.fold_in(own, 4), (count // 2,), 0, 1 << 20) % (margin + 1)
    sizes = sizes.at[donor].add(-shifted).at[receiver].add(shifted)
    items = jnp.searchsorted(jnp.cumsum(sizes), jnp.arange(rows * top), side="right").astype(jnp.int32)
    table = items.reshape(top, rows).T
    table = table[jax.random.permutation(jax.random.fold_in(own, 1), rows)]
    turn = jax.random.randint(jax.random.fold_in(own, 2), (rows, 1), 0, top)
    return jnp.take_along_axis(table, (jnp.arange(top)[None, :] + turn) % top, axis=1)


def portions_of(amount, total, most, skew, full):
    loads = [(1 << 20) // math.isqrt(grade ** skew) + 1 for grade in range(1, amount + 1)]
    largest = most if full else min(most, max(-(-total // amount), total * loads[0] // sum(loads)))
    least = 1 if total - largest >= amount - 1 else 0
    given, spare = [largest] + [least] * (amount - 1), total - largest - least * (amount - 1)
    while spare > 0:
        free = [i for i in range(1, amount) if given[i] < largest] or [i for i in range(1, amount) if given[i] < most]
        mass, budget = sum([loads[i] for i in free]), spare
        for i in free:
            extra = min(most - given[i], max(1, budget * loads[i] // mass), spare)
            given[i] = given[i] + extra
            spare = spare - extra
    return np.array(given)


def bell_draw(rng, shape, scale, limit, cuts=(), kind=jnp.bfloat16):
    values = jax.random.normal(rng, shape, jnp.float32) * scale
    if len(cuts) > 0:
        values = shard_levels(rng, shape, cuts, -0.22, 0.18) * values
    return jnp.clip(values, min=-limit, max=limit).astype(kind)


def setup_inputs(seed: int = 0) -> dict:
    key_of = jax.random.split(jax.random.key(seed), 8)
    operator = bell_draw(key_of[0], (M, M), M ** -0.5, 0.046875, ((0, 8), (1, 16)), jnp.float32)
    vectors = bell_draw(key_of[1], (M, NV), 1.0, 6.0, ((0, 8), (1, 16)), jnp.float32)
    owner_map_keys = jax.random.split(jax.random.fold_in(key_of[2], 1), OWNED // MODE_DEV)
    owner_map_turns = jax.random.permutation(jax.random.fold_in(key_of[2], 3), OWNED // MODE_DEV)
    owner_map = jax.vmap(lambda own, number: assign_block(jax.random.fold_in(key_of[2], 2), own, number, MODE_DEV, FANOUT, 1, MOST, 2))(owner_map_keys, owner_map_turns).reshape((OWNED, 1))
    coupling = bell_draw(key_of[3], (SUBS, SEPU, TOPU), TOPU ** -0.5, 0.1875, ((0, 8), (1, 16)), jnp.float32)
    ancestors = draw_ancestors(jax.random.fold_in(key_of[7], 71), 0)
    leaf_modes = bell_draw(key_of[5], (SUBS, FANOUT, INTER, MODES), MODES ** -0.5, 0.375, ((0, 8), (1, 16)), jnp.float32)
    constraint_modes = bell_draw(key_of[6], (SUBS, FANOUT, INTER, ANC), ANC ** -0.5, 0.25, ((0, 8), (1, 16)), jnp.float32)
    return {"operator": operator, "vectors": vectors, "owner_map": owner_map, "coupling": coupling, "ancestors": ancestors, "leaf_modes": leaf_modes, "constraint_modes": constraint_modes}


highest = lax.Precision.HIGHEST


def slot_ranks(owned_rows, fanout):
    onehot = (owned_rows[..., None] == jnp.arange(fanout, dtype=jnp.int32)).astype(jnp.int32)
    running = jnp.cumsum(onehot, axis=-2)
    return jnp.sum(running * onehot, axis=-1) - 1


def pick_rows(candidate_rows, index_rows):
    return jnp.take(candidate_rows, index_rows, axis=0)


def reference(operator, vectors, owner_map, coupling, ancestors, leaf_modes, constraint_modes):
    adjoint = jnp.dot(operator.T, vectors, precision=highest, preferred_element_type=jnp.float32)
    forward = jnp.dot(operator, adjoint, precision=highest, preferred_element_type=jnp.float32)
    blocks = forward.reshape(SUBS * FANOUT, ROWS_DEV, NV)
    mode_rows = blocks[:, :MODE_DEV].reshape(SUBS, FANOUT, MODE_DEV, NV)
    separator_raw = blocks[:, MODE_DEV:MODE_DEV + SEP_DEV].reshape(SUBS, SEPU, NV)
    top_rows = blocks[:, MODE_DEV + SEP_DEV:].reshape(TOPU, NV)
    owned_rows = owner_map[:, 0].reshape(SUBS, FANOUT, MODE_DEV)
    target = owned_rows * MOST + slot_ranks(owned_rows, FANOUT)
    sub_index = jnp.arange(SUBS, dtype=jnp.int32)[:, None, None]
    source_index = jnp.arange(FANOUT, dtype=jnp.int32)[None, :, None]
    buffer = jnp.zeros((SUBS, FANOUT, FANOUT * MOST, NV), jnp.float32)
    buffer = buffer.at[sub_index, source_index, target].set(mode_rows)
    coords = buffer.reshape(SUBS, FANOUT, FANOUT, MOST, NV).transpose(0, 2, 1, 3, 4).reshape(SUBS, FANOUT, MODES, NV)
    separators = separator_raw + jnp.einsum("rst,tv->rsv", coupling, top_rows, precision=highest)
    candidates = jnp.concatenate([jnp.broadcast_to(top_rows, (SUBS, TOPU, NV)), separators], axis=1)
    gathered = jax.vmap(pick_rows)(candidates, ancestors)
    interiors = jnp.einsum("rcim,rcmv->rciv", leaf_modes, coords, precision=highest)
    interiors = interiors + jnp.einsum("rcia,rcav->rciv", constraint_modes, gathered, precision=highest)
    return separators, interiors
```

```python
import jax
import jax.numpy as jnp
from jax import lax
from jax.sharding import PartitionSpec as P

highest = lax.Precision.HIGHEST


def slot_ranks(owned_rows):
    rows = owned_rows.shape[0]
    place = jnp.arange(rows, dtype=jnp.int32)
    same = (owned_rows[:, None] == owned_rows[None, :]) & (place[None, :] < place[:, None])
    return jnp.sum(same.astype(jnp.int32), axis=1)


def on_device(operator, vectors, owner_map, coupling, ancestors, leaf_modes, constraint_modes):
    fanout = lax.axis_size("col")
    mode_local = owner_map.shape[0]
    separator_local = coupling.shape[1]
    mode_count = leaf_modes.shape[3]
    slot_count = mode_count // fanout
    mode_matrix = leaf_modes[0, 0]
    partial_adjoint = lax.dot_general(
        operator,
        lax.all_gather(vectors, "col", axis=1, tiled=True),
        (((0,), (0,)), ((), ())),
        precision=highest,
        preferred_element_type=jnp.float32,
    )
    adjoint = lax.psum(partial_adjoint, "row")
    forward = jnp.dot(operator, adjoint, precision=highest, preferred_element_type=jnp.float32)
    vector_count = forward.shape[1]
    local_rows = lax.psum_scatter(forward, "col", scatter_dimension=0, tiled=True)
    mode_rows = local_rows[:mode_local]
    separator_raw = local_rows[mode_local : mode_local + separator_local]
    top_local = local_rows[mode_local + separator_local :]
    owned_here = owner_map[:, 0]
    target = owned_here * slot_count + slot_ranks(owned_here)
    source = (
        jnp.full((fanout * slot_count,), mode_local, jnp.int32)
        .at[target]
        .set(jnp.arange(mode_local, dtype=jnp.int32))
    )
    outgoing = jnp.take(mode_rows, source, axis=0, mode="fill", fill_value=0.0).reshape(
        fanout, slot_count, vector_count
    )
    received = lax.all_to_all(outgoing, "col", split_axis=0, concat_axis=0, tiled=True)
    flattened = received.reshape(mode_count, received.shape[2])
    modal_sum = jnp.dot(
        mode_matrix, flattened, precision=highest, preferred_element_type=jnp.float32
    )
    top_gathered = lax.all_gather(top_local, ("row", "col"), axis=0, tiled=True)
    separators = separator_raw + jnp.dot(
        coupling[0], top_gathered, precision=highest, preferred_element_type=jnp.float32
    )
    separator_all = lax.all_gather(separators, "col", axis=0, tiled=True)
    candidates = jnp.concatenate([top_gathered, separator_all], axis=0)
    picked = jnp.take(candidates, ancestors[0, 0], axis=0)
    interiors = modal_sum + jnp.dot(
        constraint_modes[0, 0], picked, precision=highest, preferred_element_type=jnp.float32
    )
    return (separators[None], interiors[None, None])


def solution(mesh):
    in_specs = (
        P("row", "col"),
        P("row", "col"),
        P(("row", "col"), None),
        P("row", "col", None),
        P("row", "col", None),
        P("row", "col", None, None),
        P("row", "col", None, None),
    )
    out_specs = (P("row", "col", None), P("row", "col", None, None))
    return jax.shard_map(
        on_device, mesh=mesh, in_specs=in_specs, out_specs=out_specs, check_vma=False
    )
```

```python
import functools

import jax
import jax.numpy as jnp
from jax import lax
from jax.experimental import pallas as pl
from jax.experimental.pallas import tpu as pltpu
from jax.sharding import PartitionSpec as P

MESH = pl.DeviceIdType.MESH
F32 = jnp.float32
BF16 = jnp.bfloat16
NH = 2
PLANE = [(dy, dx) for dy in range(4) for dx in range(4) if dy or dx]
N_REMOTE = 160


def split2(v):
    hi = v.astype(BF16)
    return hi, (v - hi.astype(F32)).astype(BF16)


def split3(v):
    hi = v.astype(BF16)
    rest = v - hi.astype(F32)
    mid = rest.astype(BF16)
    return hi, mid, (rest - mid.astype(F32)).astype(BF16)


def dot(a, b):
    return jnp.dot(a, b, preferred_element_type=F32)


def column_of(row):
    n = row.shape[1]
    eye = lax.broadcasted_iota(jnp.int32, (n, n), 0) == lax.broadcasted_iota(jnp.int32, (n, n), 1)
    return jnp.sum(jnp.where(eye, jnp.broadcast_to(row, (n, n)), 0.0), axis=1, keepdims=True)


def kernel(
    op_hbm, x_hbm, owner_ref, coup_ref, anc_ref, lm_hbm, cm_hbm,
    sep_out, int_hbm,
    k32, lm32, cm32, kh, kl, lmh, lml, cmh, cml,
    xg, xl, part, core_in, zsum, z_in, at, w, f,
    ra1, ra2, ra3, ra4, rb1, rb2, rb3, rb4,
    loc, own, orow, gsel, outgo, coordin, top, candt, sepall, inter,
    ss, rs, ls,
):
    row, col = lax.axis_index("row"), lax.axis_index("col")
    z, core, y, x = row // 2, row % 2, col // 4, col % 4

    def dev(dz=0, dc=0, dy=0, dx=0):
        return (((z + dz) % 4) * 2 + (core + dc) % 2, ((y + dy) % 4) * 4 + (x + dx) % 4)

    copies = []

    def send(src, dst, where):
        i = len(copies)
        c = pltpu.make_async_remote_copy(
            src_ref=src, dst_ref=dst, send_sem=ss.at[i], recv_sem=rs.at[i], device_id=where, device_id_type=MESH
        )
        c.start()
        copies.append(c)
        return c

    xp, xm, yp, ym = dev(dx=1), dev(dx=3), dev(dy=1), dev(dy=3)
    mate = dev(dc=1)

    loads = []

    def load(src, dst):
        c = pltpu.make_async_copy(src, dst, ls.at[len(loads)])
        c.start()
        loads.append(c)
        return c

    x_loads = [load(x_hbm.at[pl.ds(8 * h, 8)], xg.at[h, 0, 0]) for h in range(NH)]
    k_loads = [load(op_hbm.at[pl.ds(256 * i, 256)], k32.at[pl.ds(256 * i, 256)]) for i in range(8)]
    cm_load = load(cm_hbm, cm32)
    lm_load = load(lm_hbm, lm32)

    barrier = pltpu.get_barrier_semaphore()
    friends = [dev(dy=dy, dx=dx) for dy, dx in PLANE] + [dev(dz=d) for d in (1, 2, 3)] + [mate]
    for d in friends:
        pl.semaphore_signal(barrier, inc=1, device_id=d, device_id_type=MESH)
    pl.semaphore_wait(barrier, len(friends))
    for c in x_loads:
        c.wait()

    A, B = pl.ds(0, 1024), pl.ds(1024, 1024)
    A0, A1, B0, B1 = pl.ds(0, 512), pl.ds(512, 512), pl.ds(1024, 512), pl.ds(1536, 512)
    ag = [dict() for _ in range(NH)]

    def own_sends(h):
        s = xg.at[h, 0, 0]
        ag[h]["xp"] = send(s, xg.at[h, 0, 3], xp)
        ag[h]["xm"] = send(s, xg.at[h, 0, 1], xm)
        ag[h]["yp"] = send(s, xg.at[h, 3, 0], yp)
        ag[h]["ym"] = send(s, xg.at[h, 1, 0], ym)

    def to_y(h, dx):
        s = xg.at[h, 0, dx, :, A]
        return [send(s, xg.at[h, 3, dx, :, A], yp), send(s, xg.at[h, 1, dx, :, A], ym)]

    def to_x(h, dy):
        s = xg.at[h, dy, 0, :, B]
        return [send(s, xg.at[h, dy, 3, :, B], xp), send(s, xg.at[h, dy, 1, :, B], xm)]

    def step2(h):
        a = ag[h]
        a["xp"].wait_recv()
        a["fa"] = [send(xg.at[h, 0, 3, :, A0], xg.at[h, 0, 2, :, A0], xp)]
        a["yp"].wait_recv()
        a["fb"] = [send(xg.at[h, 3, 0, :, B0], xg.at[h, 2, 0, :, B0], yp)]
        a["xm"].wait_recv()
        a["fa"].append(send(xg.at[h, 0, 1, :, A1], xg.at[h, 0, 2, :, A1], xm))
        a["ym"].wait_recv()
        a["fb"].append(send(xg.at[h, 1, 0, :, B1], xg.at[h, 2, 0, :, B1], ym))
        a["ta"] = to_y(h, 3)
        a["tb"] = to_x(h, 3)
        a["ta"] += to_y(h, 1)
        a["tb"] += to_x(h, 1)

    def step3(h):
        a = ag[h]
        for c in a["fa"]:
            c.wait_recv()
        a["ta"] += to_y(h, 2)
        for c in a["fb"]:
            c.wait_recv()
        a["tb"] += to_x(h, 2)

    def step4(h):
        a = ag[h]
        for c in a["ta"]:
            c.wait_recv()
        a["end"] = [
            send(xg.at[h, 3, :, :, A0], xg.at[h, 2, :, :, A0], yp),
            send(xg.at[h, 1, :, :, A1], xg.at[h, 2, :, :, A1], ym),
        ]
        for c in a["tb"]:
            c.wait_recv()
        a["end"] += [
            send(xg.at[h, :, 3, :, B0], xg.at[h, :, 2, :, B0], xp),
            send(xg.at[h, :, 1, :, B1], xg.at[h, :, 2, :, B1], xm),
        ]

    def step5(h):
        for c in ag[h]["end"]:
            c.wait_recv()
        for q in range(8):
            rows = []
            for j in (2 * q, 2 * q + 1):
                rows.append(xg[h, (j // 4 + 4 - y) % 4, (j % 4 + 4 - x) % 4])
            hi, lo = split2(jnp.concatenate(rows, axis=0))
            xl[h, pl.ds(16 * q, 16), :] = hi
            xl[h, pl.ds(128 + 16 * q, 16), :] = lo

    def split_k(i):
        k_loads[i].wait()

        @pl.loop(0, 8)
        def _(j):
            r = pl.ds(pl.multiple_of(256 * i + 32 * j, 32), 32)
            hi, lo = split2(k32[r, :])
            kh[r, :] = hi
            kl[r, :] = lo

    def mm1(h, n):
        c = pl.ds(256 * n, 256)
        p = dot(xl[h], kh[:, c])
        p = p[:128] + p[128:] + dot(xl[h, 0:128], kl[:, c])
        part[h, :, :, :, c] = p.reshape(2, 4, 16, 256)

    ar = [dict() for _ in range(NH)]

    def ar1(h):
        ar[h]["c"] = send(part.at[h, 1 - core], core_in.at[h], mate)

    def ar2(h):
        ar[h]["c"].wait_recv()
        zsum[h] = part[h, core] + core_in[h]
        ar[h]["z"] = [send(zsum.at[h, (z + d) % 4], z_in.at[h, d - 1], dev(dz=d)) for d in (2, 1, 3)]

    def ar3(h):
        for c in ar[h]["z"]:
            c.wait_recv()
        at[h, core, z] = zsum[h, z] + z_in[h, 0] + z_in[h, 1] + z_in[h, 2]
        s = at.at[h, core, z]
        ar[h]["g"] = [(d, send(s, s, dev(dz=d))) for d in (2, 1, 3)]
        ar[h]["m"] = [send(s, s, mate)]

    def ar4(h):
        for d, c in sorted(ar[h]["g"], key=lambda t: t[0] % 2 == 0):
            c.wait_recv()
            s = at.at[h, core, (z + 4 - d) % 4]
            ar[h]["m"].append(send(s, s, mate))

    def ar5(h):
        for c in ar[h]["m"]:
            c.wait_recv()
        for n in range(8):
            c = pl.ds(128 * n, 128)
            hi, lo = split2(at[h, :, :, :, c].reshape(128, 128).T)
            w[h, c, 0:128] = hi
            w[h, c, 128:256] = lo

    def mm2(h, slots):
        for dy, dx in slots:
            b = ((y + dy) % 4) * 4 + (x + dx) % 4
            r = pl.ds(pl.multiple_of(b * 128, 128), 128)
            p = dot(kh[r, :], w[h])
            f[h, dy, dx] = p[:, :128] + p[:, 128:] + dot(kl[r, :], w[h, :, 0:128])

    rc = [dict() for _ in range(NH)]
    lo32, hi32, lo64 = pl.ds(0, 32), pl.ds(32, 32), pl.ds(0, 64)
    lo32b, hi32b, hi64 = pl.ds(64, 32), pl.ds(96, 32), pl.ds(64, 64)

    def rs1(h):
        mm2(h, [(dy, 2) for dy in range(4)])
        rc[h]["a1"] = [
            send(f.at[h, :, 2, lo32], ra1.at[h, 0], xp),
            send(f.at[h, :, 2, hi32], ra1.at[h, 1], xm),
        ]
        mm2(h, [(2, dx) for dx in (0, 1, 3)])
        rc[h]["b1"] = [
            send(f.at[h, 2, :, lo32b], rb1.at[h, 0], yp),
            send(f.at[h, 2, :, hi32b], rb1.at[h, 1], ym),
        ]
        mm2(h, [(1, 1), (3, 1), (0, 1), (1, 3), (3, 3), (0, 3), (1, 0), (3, 0), (0, 0)])

    def rs2(h):
        for c in rc[h]["a1"]:
            c.wait_recv()
        f[h, :, 1, 0:32] += ra1[h, 0]
        f[h, :, 3, 32:64] += ra1[h, 1]
        rc[h]["a2"] = [
            send(f.at[h, :, 1, lo64], ra2.at[h, 0], xp),
            send(f.at[h, :, 3, lo64], ra2.at[h, 1], xm),
        ]
        for c in rc[h]["b1"]:
            c.wait_recv()
        f[h, 1, :, 64:96] += rb1[h, 0]
        f[h, 3, :, 96:128] += rb1[h, 1]
        rc[h]["b2"] = [
            send(f.at[h, 1, :, hi64], rb2.at[h, 0], yp),
            send(f.at[h, 3, :, hi64], rb2.at[h, 1], ym),
        ]

    def rs3(h):
        for c in rc[h]["a2"]:
            c.wait_recv()
        f[h, :, 0, 0:64] += ra2[h, 0] + ra2[h, 1]
        rc[h]["a3"] = [
            send(f.at[h, 2, 0, lo32], ra3.at[h, 0], yp),
            send(f.at[h, 2, 0, hi32], ra3.at[h, 1], ym),
        ]
        for c in rc[h]["b2"]:
            c.wait_recv()
        f[h, 0, :, 64:128] += rb2[h, 0] + rb2[h, 1]
        rc[h]["b3"] = [
            send(f.at[h, 0, 2, lo32b], rb3.at[h, 0], xp),
            send(f.at[h, 0, 2, hi32b], rb3.at[h, 1], xm),
        ]

    def rs4(h):
        for c in rc[h]["a3"]:
            c.wait_recv()
        f[h, 1, 0, 0:32] += ra3[h, 0]
        f[h, 3, 0, 32:64] += ra3[h, 1]
        rc[h]["a4"] = [
            send(f.at[h, 1, 0, lo64], ra4.at[h, 0], yp),
            send(f.at[h, 3, 0, lo64], ra4.at[h, 1], ym),
        ]
        for c in rc[h]["b3"]:
            c.wait_recv()
        f[h, 0, 1, 64:96] += rb3[h, 0]
        f[h, 0, 3, 96:128] += rb3[h, 1]
        rc[h]["b4"] = [
            send(f.at[h, 0, 1, hi64], rb4.at[h, 0], xp),
            send(f.at[h, 0, 3, hi64], rb4.at[h, 1], xm),
        ]

    def rs5(h):
        for c in rc[h]["a4"] + rc[h]["b4"]:
            c.wait_recv()
        c = pl.ds(128 * h, 128)
        loc[0:64, c] = f[h, 0, 0, 0:64] + ra4[h, 0] + ra4[h, 1]
        loc[64:128, c] = f[h, 0, 0, 64:128] + rb4[h, 0] + rb4[h, 1]

    def select_modes():
        orow[...] = jnp.full((1, 128), -1.0, F32)
        orow[:, 0:88] = owner_ref[...].astype(F32)
        r = orow[...]
        c = column_of(r)
        q, p = lax.broadcasted_iota(jnp.int32, (128, 128), 0), lax.broadcasted_iota(jnp.int32, (128, 128), 1)
        rank = jnp.sum(jnp.where((c == r) & (q < p), 1.0, 0.0), axis=0, keepdims=True)
        target = jnp.where(r < 0.0, -1.0, r * 16.0 + rank)
        slot = lax.broadcasted_iota(jnp.int32, (256, 128), 0).astype(F32)
        own[...] = jnp.where(slot == target, 1.0, 0.0).astype(BF16)

    def select_ancestors():
        for i in range(4):
            c = column_of(anc_ref[:, pl.ds(128 * i, 128)].astype(F32))
            for j in range(3):
                place = lax.broadcasted_iota(jnp.int32, (128, 512), 1).astype(F32) + 512.0 * j
                gsel[pl.ds(128 * i, 128), pl.ds(512 * j, 512)] = jnp.where(c == place, 1.0, 0.0).astype(BF16)

    def split_rows(src, hi_ref, lo_ref, rows):
        @pl.loop(0, 2048 // rows)
        def _(j):
            r = pl.ds(pl.multiple_of(rows * j, rows), rows)
            hi, lo = split2(src[r, :])
            hi_ref[r, :] = hi
            lo_ref[r, :] = lo

    own_sends(0)
    own_sends(1)
    split_k(0)
    split_k(1)
    step2(0)
    split_k(2)
    step2(1)
    split_k(3)
    step3(0)
    split_k(4)
    step3(1)
    split_k(5)
    step4(0)
    split_k(6)
    split_k(7)
    step5(0)
    mm1(0, 0)
    mm1(0, 1)
    step4(1)
    mm1(0, 2)
    mm1(0, 3)
    ar1(0)
    step5(1)
    ar2(0)
    mm1(1, 0)
    mm1(1, 1)
    mm1(1, 2)
    mm1(1, 3)
    ar1(1)
    ar3(0)
    ar2(1)
    select_modes()
    select_ancestors()
    ar4(0)
    ar5(0)
    ar3(1)
    rs1(0)
    ar4(1)
    rs2(0)
    ar5(1)
    rs3(0)
    rs1(1)
    rs4(0)
    rs2(1)
    rs5(0)
    cm_load.wait()
    split_rows(cm32, cmh, cml, 32)
    rs3(1)
    lm_load.wait()
    split_rows(lm32, lmh, lml, 64)
    rs4(1)
    rs5(1)

    pv, pp = lax.broadcasted_iota(jnp.int32, (256, 256), 1), lax.broadcasted_iota(jnp.int32, (256, 256), 0)
    order = jnp.where(pp == ((pv // 8) % 2) * 128 + (pv // 16) * 8 + pv % 8, 1.0, 0.0).astype(BF16)
    a, b, c = split3(loc[...])
    mine = dot(a, order) + dot(b, order) + dot(c, order)

    top[z, core, col] = mine[120:128]
    s = top.at[z, core, col]
    tz = [send(s, s, dev(dz=d)) for d in (2, 1, 3)]

    hi, lo = split2(mine)
    out = dot(own[...], hi) + dot(own[...], lo)
    outgo[...] = out.reshape(16, 16, 256)
    coordin[col] = outgo[col]

    for t in tz:
        t.wait_recv()
    s = top.at[:, core, col]
    tp = [send(s, s, dev(dy=dy, dx=dx)) for dy, dx in PLANE]
    mx = []
    for dy, dx in PLANE:
        d = dev(dy=dy, dx=dx)
        mx.append(send(outgo.at[d[1]], coordin.at[col], d))
    ch, cl = split2(coup_ref[...])
    cc = jnp.concatenate([ch, cl], axis=0)
    for t in tp:
        t.wait_recv()
    s = top.at[:, core]
    tc = send(s, s, mate)
    tc.wait_recv()
    hi, lo = split2(top[...].reshape(1024, 256))
    candt[:, 0:256] = hi
    candt[:, 256:512] = lo
    p = dot(cc, hi)
    sep = mine[88:120] + (p[:32] + p[32:] + dot(ch, lo))
    sep_out[...] = sep
    sepall[col] = sep
    s = sepall.at[col]
    se = [send(s, s, dev(dy=dy, dx=dx)) for dy, dx in PLANE]
    gath = dot(gsel[:, 0:1024], candt[...])
    for t in mx:
        t.wait_recv()
    hi, lo = split2(coordin[...].reshape(256, 256))
    for i in range(4):
        r = pl.ds(512 * i, 512)
        inter[r, :] = dot(lmh[r, :], hi) + dot(lmh[r, :], lo) + dot(lml[r, :], hi)
    for t in se:
        t.wait_recv()
    hi, lo = split2(sepall[...].reshape(512, 256))
    gath = gath + dot(gsel[:, 1024:1536], jnp.concatenate([hi, lo], axis=1))
    hi, lo = gath[:, :256].astype(BF16), gath[:, 256:].astype(BF16)
    outs = []
    for i in range(4):
        r = pl.ds(512 * i, 512)
        inter[r, :] += dot(cmh[r, :], hi) + dot(cmh[r, :], lo) + dot(cml[r, :], hi)
        outs.append(load(inter.at[r], int_hbm.at[r]))
    for t in outs:
        t.wait()
    for t in copies:
        t.wait_send()


def on_device(operator, vectors, owner_map, coupling, ancestors, leaf_modes, constraint_modes):
    vmem, anywhere = pl.BlockSpec(memory_space=pltpu.VMEM), pl.BlockSpec(memory_space=pl.ANY)
    scratch = [
        ((2048, 1024), F32), ((2048, 256), F32), ((2048, 512), F32),
        ((2048, 1024), BF16), ((2048, 1024), BF16),
        ((2048, 256), BF16), ((2048, 256), BF16), ((2048, 512), BF16), ((2048, 512), BF16),
        ((NH, 4, 4, 8, 2048), F32), ((NH, 256, 2048), BF16),
        ((NH, 2, 4, 16, 1024), F32), ((NH, 4, 16, 1024), F32),
        ((NH, 4, 16, 1024), F32), ((NH, 3, 16, 1024), F32), ((NH, 2, 4, 16, 1024), F32),
        ((NH, 1024, 256), BF16), ((NH, 4, 4, 128, 128), F32),
        ((NH, 2, 4, 32, 128), F32), ((NH, 2, 4, 64, 128), F32), ((NH, 2, 32, 128), F32), ((NH, 2, 64, 128), F32),
        ((NH, 2, 4, 32, 128), F32), ((NH, 2, 4, 64, 128), F32), ((NH, 2, 32, 128), F32), ((NH, 2, 64, 128), F32),
        ((128, 256), F32), ((256, 128), BF16), ((1, 128), F32), ((512, 1536), BF16),
        ((16, 16, 256), F32), ((16, 16, 256), F32), ((4, 2, 16, 8, 256), F32),
        ((1024, 512), BF16), ((16, 32, 256), F32), ((2048, 256), F32),
    ]
    separators, interiors = pl.pallas_call(
        kernel,
        out_shape=(jax.ShapeDtypeStruct((32, 256), F32), jax.ShapeDtypeStruct((2048, 256), F32)),
        in_specs=[anywhere, anywhere, vmem, vmem, vmem, anywhere, anywhere],
        out_specs=(vmem, anywhere),
        scratch_shapes=[pltpu.VMEM(s, t) for s, t in scratch]
        + [pltpu.SemaphoreType.DMA((N_REMOTE,)), pltpu.SemaphoreType.DMA((N_REMOTE,)), pltpu.SemaphoreType.DMA((16,))],
        compiler_params=pltpu.CompilerParams(collective_id=0, has_side_effects=True, vmem_limit_bytes=61 << 20),
        cost_estimate=pl.CostEstimate(flops=9_000_000_000, bytes_accessed=20_000_000, transcendentals=0),
        name="step",
    )(
        operator, vectors.T, owner_map.reshape(1, 88), coupling[0], ancestors[0],
        leaf_modes[0, 0], constraint_modes[0, 0],
    )
    return separators[None], interiors[None, None]


def solution(mesh):
    in_specs = (
        P("row", "col"),
        P("row", "col"),
        P(("row", "col"), None),
        P("row", "col", None),
        P("row", "col", None),
        P("row", "col", None, None),
        P("row", "col", None, None),
    )
    out_specs = (P("row", "col", None), P("row", "col", None, None))
    return jax.shard_map(
        on_device, mesh=mesh, in_specs=in_specs, out_specs=out_specs, check_vma=False
    )
```

```python
import functools

import jax
import jax.numpy as jnp
from jax import lax
from jax.experimental import pallas as pl
from jax.experimental.pallas import tpu as pltpu
from jax.sharding import PartitionSpec as P

MESH = pl.DeviceIdType.MESH
F32 = jnp.float32
BF16 = jnp.bfloat16
NH = 2
PLANE = [(dy, dx) for dy in range(4) for dx in range(4) if dy or dx]
N_REMOTE = 200
STOP = None
FAR_FIRST = sorted(PLANE, key=lambda p: -min(p[0], 4 - p[0]) - min(p[1], 4 - p[1]))
VMEM_STEP = 57 << 20


def split2(v):
    hi = v.astype(BF16)
    return hi, (v - hi.astype(F32)).astype(BF16)


def split3(v):
    hi = v.astype(BF16)
    rest = v - hi.astype(F32)
    mid = rest.astype(BF16)
    return hi, mid, (rest - mid.astype(F32)).astype(BF16)


def dot(a, b):
    return jnp.dot(a, b, preferred_element_type=F32)


def column_of(row):
    n = row.shape[1]
    eye = lax.broadcasted_iota(jnp.int32, (n, n), 0) == lax.broadcasted_iota(jnp.int32, (n, n), 1)
    return jnp.sum(jnp.where(eye, jnp.broadcast_to(row, (n, n)), 0.0), axis=1, keepdims=True)


class Sent:
    def __init__(self, copy):
        self.copy, self.landed = copy, False

    def wait_recv(self):
        if not self.landed:
            self.copy.wait_recv()
        self.landed = True


class Loaded:
    def __init__(self, copy):
        self.copy, self.landed = copy, False

    def wait(self):
        if not self.landed:
            self.copy.wait()
        self.landed = True


def kernel(
    op_hbm, x_hbm, owner_ref, coup_ref, anc_ref,
    sep_out, gath_out, coord_out,
    k32, kh, kl, xg, xl, part, core_in, zsum, z_in, at, w, f,
    ra1, ra2, ra3, rb1, rb2, rb3,
    loc, own, orow, gsel, outgo, coordin, top, cc, sepall,
    ss, rs, ls,
):
    row, col = lax.axis_index("row"), lax.axis_index("col")
    z, core, y, x = row // 2, row % 2, col // 4, col % 4

    def dev(dz=0, dc=0, dy=0, dx=0):
        return (((z + dz) % 4) * 2 + (core + dc) % 2, ((y + dy) % 4) * 4 + (x + dx) % 4)

    copies = []

    def send(src, dst, where):
        i = len(copies)
        c = pltpu.make_async_remote_copy(
            src_ref=src, dst_ref=dst, send_sem=ss.at[i], recv_sem=rs.at[i], device_id=where, device_id_type=MESH
        )
        c.start()
        copies.append(Sent(c))
        return copies[-1]

    xp, xm, yp, ym = dev(dx=1), dev(dx=3), dev(dy=1), dev(dy=3)
    mate = dev(dc=1)

    loads = []

    def load(src, dst):
        c = pltpu.make_async_copy(src, dst, ls.at[len(loads)])
        c.start()
        loads.append(Loaded(c))
        return loads[-1]

    x_loads = [load(x_hbm.at[pl.ds(8 * h, 8)], xg.at[h, 0, 0]) for h in range(NH)]
    k_loads = [load(op_hbm.at[pl.ds(256 * i, 256)], k32.at[pl.ds(256 * i, 256)]) for i in range(8)]
    barrier = pltpu.get_barrier_semaphore()
    friends = [dev(dy=dy, dx=dx) for dy, dx in PLANE] + [dev(dz=d) for d in (1, 2, 3)] + [mate]
    for d in friends:
        pl.semaphore_signal(barrier, inc=1, device_id=d, device_id_type=MESH)
    pl.semaphore_wait(barrier, len(friends))
    for c in x_loads:
        c.wait()

    A, B = pl.ds(0, 1024), pl.ds(1024, 1024)
    A0, A1, B0, B1 = pl.ds(0, 512), pl.ds(512, 512), pl.ds(1024, 512), pl.ds(1536, 512)
    ag = [dict() for _ in range(NH)]

    def own_sends(h):
        s, a = xg.at[h, 0, 0], ag[h]
        a["xp"] = send(s, xg.at[h, 0, 3], xp)
        a["xm"] = send(s, xg.at[h, 0, 1], xm)
        a["yp"] = send(s, xg.at[h, 3, 0], yp)
        a["ym"] = send(s, xg.at[h, 1, 0], ym)
        a["xo"] = send(xg.at[h, 0, 0, :, A], xg.at[h, 0, 2, :, A], dev(dx=2))
        a["yo"] = send(xg.at[h, 0, 0, :, B], xg.at[h, 2, 0, :, B], dev(dy=2))

    def to_y(h, dx):
        s = xg.at[h, 0, dx, :, A]
        return [send(s, xg.at[h, 3, dx, :, A], yp), send(s, xg.at[h, 1, dx, :, A], ym)]

    def to_x(h, dy):
        s = xg.at[h, dy, 0, :, B]
        return [send(s, xg.at[h, dy, 3, :, B], xp), send(s, xg.at[h, dy, 1, :, B], xm)]

    def step2(h):
        a = ag[h]
        a["ta"], a["tb"] = [], []
        a["xp"].wait_recv()
        a["ta"] += to_y(h, 3)
        a["yp"].wait_recv()
        a["tb"] += to_x(h, 3)
        a["xm"].wait_recv()
        a["ta"] += to_y(h, 1)
        a["ym"].wait_recv()
        a["tb"] += to_x(h, 1)

    def step3(h):
        a = ag[h]
        a["xo"].wait_recv()
        a["ta"] += to_y(h, 2)
        a["yo"].wait_recv()
        a["tb"] += to_x(h, 2)

    def step4(h):
        a = ag[h]
        for c in a["ta"]:
            c.wait_recv()
        a["end"] = [
            send(xg.at[h, 3, :, :, A0], xg.at[h, 2, :, :, A0], yp),
            send(xg.at[h, 1, :, :, A1], xg.at[h, 2, :, :, A1], ym),
        ]
        for c in a["tb"]:
            c.wait_recv()
        a["end"] += [
            send(xg.at[h, :, 3, :, B0], xg.at[h, :, 2, :, B0], xp),
            send(xg.at[h, :, 1, :, B1], xg.at[h, :, 2, :, B1], xm),
        ]

    def step5(h):
        for c in ag[h]["end"]:
            c.wait_recv()
        for q in range(8):
            rows = []
            for j in (2 * q, 2 * q + 1):
                rows.append(xg[h, (j // 4 + 4 - y) % 4, (j % 4 + 4 - x) % 4])
            hi, lo = split2(jnp.concatenate(rows, axis=0))
            xl[h, pl.ds(16 * q, 16), :] = hi
            xl[h, pl.ds(128 + 16 * q, 16), :] = lo

    def split_k(i):
        k_loads[i].wait()

        @pl.loop(0, 8)
        def _(j):
            r = pl.ds(pl.multiple_of(256 * i + 32 * j, 32), 32)
            hi, lo = split2(k32[r, :])
            kh[r, :] = hi
            kl[r, :] = lo

    def mm1(h, n):
        c = pl.ds(256 * n, 256)
        p = dot(xl[h], kh[:, c])
        p = p[:128] + p[128:] + dot(xl[h, 0:128], kl[:, c])
        part[h, :, :, :, c] = p.reshape(2, 4, 16, 256)

    ar = [dict() for _ in range(NH)]

    def ar1(h):
        ar[h]["c"] = send(part.at[h, 1 - core], core_in.at[h], mate)

    def ar2(h):
        ar[h]["c"].wait_recv()
        zsum[h] = part[h, core] + core_in[h]
        ar[h]["z"] = [send(zsum.at[h, (z + d) % 4], z_in.at[h, d - 1], dev(dz=d)) for d in (2, 1, 3)]

    def ar3(h):
        for c in ar[h]["z"]:
            c.wait_recv()
        at[h, core, z] = zsum[h, z] + z_in[h, 0] + z_in[h, 1] + z_in[h, 2]
        s = at.at[h, core, z]
        ar[h]["g"] = [(d, send(s, s, dev(dz=d))) for d in (2, 1, 3)]
        ar[h]["m"] = [send(s, s, mate)]

    def ar4(h):
        for d, c in sorted(ar[h]["g"], key=lambda t: t[0] % 2 == 0):
            c.wait_recv()
            s = at.at[h, core, (z + 4 - d) % 4]
            ar[h]["m"].append(send(s, s, mate))

    def ar5(h):
        for c in ar[h]["m"]:
            c.wait_recv()
        for n in range(8):
            c = pl.ds(128 * n, 128)
            hi, lo = split2(at[h, :, :, :, c].reshape(128, 128).T)
            w[h, c, 0:128] = hi
            w[h, c, 128:256] = lo

    def mm2(h, slots):
        for dy, dx in slots:
            b = ((y + dy) % 4) * 4 + (x + dx) % 4
            r = pl.ds(pl.multiple_of(b * 128, 128), 128)
            p = dot(kh[r, :], w[h])
            f[h, dy, dx] = p[:, :128] + p[:, 128:] + dot(kl[r, :], w[h, :, 0:128])

    rc = [dict() for _ in range(NH)]
    lo32, hi32, lo64 = pl.ds(0, 32), pl.ds(32, 32), pl.ds(0, 64)
    lo32b, hi32b, hi64 = pl.ds(64, 32), pl.ds(96, 32), pl.ds(64, 64)

    def rs1(h):
        mm2(h, [(dy, 2) for dy in range(4)])
        rc[h]["a1"] = [
            send(f.at[h, :, 2, lo32], ra1.at[h, 0], xp),
            send(f.at[h, :, 2, hi32], ra1.at[h, 1], xm),
        ]
        mm2(h, [(2, dx) for dx in (0, 1, 3)])
        rc[h]["b1"] = [
            send(f.at[h, 2, :, lo32b], rb1.at[h, 0], yp),
            send(f.at[h, 2, :, hi32b], rb1.at[h, 1], ym),
        ]
        mm2(h, [(1, 1), (3, 1), (0, 1), (1, 3), (3, 3), (0, 3), (1, 0), (3, 0), (0, 0)])

    def rs2(h):
        for c in rc[h]["a1"]:
            c.wait_recv()
        f[h, :, 1, 0:32] += ra1[h, 0]
        f[h, :, 3, 32:64] += ra1[h, 1]
        rc[h]["a2"] = [
            send(f.at[h, :, 1, lo64], ra2.at[h, 0], xp),
            send(f.at[h, :, 3, lo64], ra2.at[h, 1], xm),
        ]
        for c in rc[h]["b1"]:
            c.wait_recv()
        f[h, 1, :, 64:96] += rb1[h, 0]
        f[h, 3, :, 96:128] += rb1[h, 1]
        rc[h]["b2"] = [
            send(f.at[h, 1, :, hi64], rb2.at[h, 0], yp),
            send(f.at[h, 3, :, hi64], rb2.at[h, 1], ym),
        ]

    def rs3(h):
        for c in rc[h]["a2"]:
            c.wait_recv()
        f[h, :, 0, 0:64] += ra2[h, 0] + ra2[h, 1]
        rc[h]["a3"] = [send(f.at[h, d, 0, lo64], ra3.at[h, d - 1], dev(dy=d)) for d in (2, 1, 3)]
        for c in rc[h]["b2"]:
            c.wait_recv()
        f[h, 0, :, 64:128] += rb2[h, 0] + rb2[h, 1]
        rc[h]["b3"] = [send(f.at[h, 0, d, hi64], rb3.at[h, d - 1], dev(dx=d)) for d in (2, 1, 3)]

    def rs5(h):
        for c in rc[h]["b3"]:
            c.wait_recv()
        loc[h, 64:128] = f[h, 0, 0, 64:128] + rb3[h, 0] + rb3[h, 1] + rb3[h, 2]

    def rs6(h):
        for c in rc[h]["a3"]:
            c.wait_recv()
        loc[h, 0:64] = f[h, 0, 0, 0:64] + ra3[h, 0] + ra3[h, 1] + ra3[h, 2]

    def select_modes():
        orow[...] = jnp.full((1, 128), -1.0, F32)
        orow[:, 0:88] = owner_ref[...].astype(F32)
        r = orow[...]
        c = column_of(r)
        q, p = lax.broadcasted_iota(jnp.int32, (128, 128), 0), lax.broadcasted_iota(jnp.int32, (128, 128), 1)
        rank = jnp.sum(jnp.where((c == r) & (q < p), 1.0, 0.0), axis=0, keepdims=True)
        target = jnp.where(r < 0.0, -1.0, r * 16.0 + rank)
        slot = lax.broadcasted_iota(jnp.int32, (256, 128), 0).astype(F32)
        own[...] = jnp.where(slot == target, 1.0, 0.0).astype(BF16)

    def select_ancestors():
        for i in range(4):
            c = column_of(anc_ref[:, pl.ds(128 * i, 128)].astype(F32))
            for j in range(3):
                place = lax.broadcasted_iota(jnp.int32, (128, 512), 1).astype(F32) + 512.0 * j
                gsel[pl.ds(128 * i, 128), pl.ds(512 * j, 512)] = jnp.where(c == place, 1.0, 0.0).astype(BF16)

    t = [dict() for _ in range(NH)]

    def top_z(h):
        top[h, z, core, col] = loc[h, 120:128]
        s = top.at[h, z, core, col]
        t[h]["tz"] = [send(s, s, dev(dz=d)) for d in (2, 1, 3)]

    def top_plane(h):
        for c in t[h]["tz"]:
            c.wait_recv()
        s = top.at[h, :, core, col]
        t[h]["tp"] = [send(s, s, dev(dy=dy, dx=dx)) for dy, dx in FAR_FIRST]

    def mode_send(h):
        hi, lo = split2(loc[h])
        out = dot(own[...], jnp.concatenate([hi, lo], axis=1))
        outgo[h] = (out[:, :128] + out[:, 128:]).reshape(16, 16, 128)
        coordin[h, col] = outgo[h, col]
        t[h]["mx"] = []
        for dy, dx in FAR_FIRST:
            d = dev(dy=dy, dx=dx)
            t[h]["mx"].append(send(outgo.at[h, d[1]], coordin.at[h, col], d))

    def top_core(h):
        for c in t[h]["tp"]:
            c.wait_recv()
        s = top.at[h, :, core]
        t[h]["tc"] = send(s, s, mate)

    def split_coupling():
        ch, cl = split2(coup_ref[...])
        cc[0:32, :] = ch
        cc[32:64, :] = cl

    def separators(h):
        t[h]["tc"].wait_recv()
        hi, lo = split2(top[h].reshape(1024, 128))
        c = jnp.concatenate([hi, lo], axis=1)
        p = dot(cc[...], c)
        sep = loc[h, 88:120] + (p[:32, :128] + p[:32, 128:] + p[32:, :128])
        sep_out[h] = sep
        sepall[h, col] = sep
        s = sepall.at[h, col]
        t[h]["se"] = [send(s, s, dev(dy=dy, dx=dx)) for dy, dx in FAR_FIRST]
        t[h]["cand"] = c

    def gather_top(h):
        t[h]["gath"] = dot(gsel[:, 0:1024], t[h]["cand"])

    def mode_recv(h):
        for c in t[h]["mx"]:
            c.wait_recv()
        coord_out[h] = coordin[h].reshape(256, 128)

    def gather_sep(h):
        for c in t[h]["se"]:
            c.wait_recv()
        hi, lo = split2(sepall[h].reshape(512, 128))
        gath = t[h]["gath"] + dot(gsel[:, 1024:1536], jnp.concatenate([hi, lo], axis=1))
        gath_out[h] = gath.astype(BF16)

    def sent():
        for c in copies:
            c.wait_recv()
            c.copy.wait_send()
        for c in loads:
            c.wait()

    program = [
        (own_sends, 0), (own_sends, 1), (select_modes,), (select_ancestors,), (split_coupling,),
        (step2, 0), (step3, 0), (split_k, 0), (split_k, 1), (split_k, 2), (split_k, 3), (step2, 1), (step3, 1),
        (split_k, 4), (split_k, 5), (split_k, 6), (split_k, 7), (step4, 0), (step4, 1), (step5, 0),
        (mm1, 0, 0), (mm1, 0, 1), (mm1, 0, 2), (mm1, 0, 3), (ar1, 0), (ar2, 0), (step5, 1),
        (mm1, 1, 0), (mm1, 1, 1), (mm1, 1, 2), (mm1, 1, 3), (ar1, 1), (ar2, 1), (ar3, 0),
        (ar4, 0), (ar3, 1), (ar5, 0), (rs1, 0), (ar4, 1), (rs2, 0), (ar5, 1), (rs1, 1), (rs3, 0), (rs2, 1),
        (rs5, 0), (top_z, 0), (rs6, 0), (rs3, 1), (top_plane, 0), (mode_send, 0), (rs5, 1), (top_z, 1), (rs6, 1),
        (top_plane, 1), (top_core, 0), (mode_send, 1), (separators, 0), (top_core, 1), (gather_top, 0),
        (separators, 1), (gather_top, 1), (gather_sep, 0), (mode_recv, 0), (mode_recv, 1), (gather_sep, 1),
    ]
    for step, *args in program[:STOP] + [(sent,)]:
        step(*args)


def last(cm_ref, lm_ref, sep_ref, gath_ref, coord_ref, sep_out, int_out, gh, gl, ch, cl):
    @pl.when(pl.program_id(0) == 0)
    def _():
        pv, pp = lax.broadcasted_iota(jnp.int32, (256, 256), 1), lax.broadcasted_iota(jnp.int32, (256, 256), 0)
        order = jnp.where(pp == ((pv // 8) % 2) * 128 + (pv // 16) * 8 + pv % 8, 1.0, 0.0).astype(BF16)
        a, b, c = split3(jnp.concatenate([sep_ref[0], sep_ref[1]], axis=1))
        sep_out[...] = dot(a, order) + dot(b, order) + dot(c, order)
        gh[...] = dot(jnp.concatenate([gath_ref[0, :, 0:128], gath_ref[1, :, 0:128]], axis=1), order).astype(BF16)
        gl[...] = dot(jnp.concatenate([gath_ref[0, :, 128:256], gath_ref[1, :, 128:256]], axis=1), order).astype(BF16)
        a, b = split2(jnp.concatenate([coord_ref[0], coord_ref[1]], axis=1))
        ch[...] = dot(a, order).astype(BF16)
        cl[...] = dot(b, order).astype(BF16)

    mh, ml = split2(cm_ref[...])
    total = dot(mh, gh[...]) + dot(mh, gl[...]) + dot(ml, gh[...])
    mh, ml = split2(lm_ref[...])
    int_out[...] = total + (dot(mh, ch[...]) + dot(mh, cl[...]) + dot(ml, ch[...]))


def on_device(operator, vectors, owner_map, coupling, ancestors, leaf_modes, constraint_modes):
    vmem, anywhere = pl.BlockSpec(memory_space=pltpu.VMEM), pl.BlockSpec(memory_space=pl.ANY)
    scratch = [
        ((2048, 1024), F32), ((2048, 1024), BF16), ((2048, 1024), BF16),
        ((NH, 4, 4, 8, 2048), F32), ((NH, 256, 2048), BF16),
        ((NH, 2, 4, 16, 1024), F32), ((NH, 4, 16, 1024), F32),
        ((NH, 4, 16, 1024), F32), ((NH, 3, 16, 1024), F32), ((NH, 2, 4, 16, 1024), F32),
        ((NH, 1024, 256), BF16), ((NH, 4, 4, 128, 128), F32),
        ((NH, 2, 4, 32, 128), F32), ((NH, 2, 4, 64, 128), F32), ((NH, 3, 64, 128), F32),
        ((NH, 2, 4, 32, 128), F32), ((NH, 2, 4, 64, 128), F32), ((NH, 3, 64, 128), F32),
        ((NH, 128, 128), F32), ((256, 128), BF16), ((1, 128), F32), ((512, 1536), BF16),
        ((NH, 16, 16, 128), F32), ((NH, 16, 16, 128), F32), ((NH, 4, 2, 16, 8, 128), F32),
        ((64, 1024), BF16), ((NH, 16, 32, 128), F32),
    ]
    sep, gath, coords = pl.pallas_call(
        kernel,
        out_shape=(
            jax.ShapeDtypeStruct((NH, 32, 128), F32),
            jax.ShapeDtypeStruct((NH, 512, 256), BF16),
            jax.ShapeDtypeStruct((NH, 256, 128), F32),
        ),
        in_specs=[anywhere, anywhere, vmem, vmem, vmem],
        out_specs=(vmem, vmem, vmem),
        scratch_shapes=[pltpu.VMEM(s, t) for s, t in scratch]
        + [pltpu.SemaphoreType.DMA((N_REMOTE,)), pltpu.SemaphoreType.DMA((N_REMOTE,)), pltpu.SemaphoreType.DMA((16,))],
        compiler_params=pltpu.CompilerParams(collective_id=0, has_side_effects=True, vmem_limit_bytes=VMEM_STEP),
        cost_estimate=pl.CostEstimate(flops=9_000_000_000, bytes_accessed=20_000_000, transcendentals=0),
        name="step",
    )(operator, vectors.T, owner_map.reshape(1, 88), coupling[0], ancestors[0])

    def whole(*shape):
        return pl.BlockSpec(shape, lambda i: (0,) * len(shape))

    def rows(width):
        return pl.BlockSpec((512, width), lambda i: (i, 0))

    separators, interiors = pl.pallas_call(
        last,
        grid=(4,),
        out_shape=(jax.ShapeDtypeStruct((32, 256), F32), jax.ShapeDtypeStruct((2048, 256), F32)),
        in_specs=[rows(512), rows(256), whole(NH, 32, 128), whole(NH, 512, 256), whole(NH, 256, 128)],
        out_specs=(whole(32, 256), rows(256)),
        scratch_shapes=[pltpu.VMEM(s, BF16) for s in ((512, 256), (512, 256), (256, 256), (256, 256))],
        compiler_params=pltpu.CompilerParams(vmem_limit_bytes=57 << 20),
        name="last",
    )(constraint_modes[0, 0], leaf_modes[0, 0], sep, gath, coords)
    return separators[None], interiors[None, None]


def solution(mesh):
    in_specs = (
        P("row", "col"),
        P("row", "col"),
        P(("row", "col"), None),
        P("row", "col", None),
        P("row", "col", None),
        P("row", "col", None, None),
        P("row", "col", None, None),
    )
    out_specs = (P("row", "col", None), P("row", "col", None, None))
    return jax.shard_map(
        on_device, mesh=mesh, in_specs=in_specs, out_specs=out_specs, check_vma=False
    )
```

```python
import functools

import jax
import jax.numpy as jnp
from jax import lax
from jax.experimental import pallas as pl
from jax.experimental.pallas import tpu as pltpu
from jax.sharding import PartitionSpec as P

MESH = pl.DeviceIdType.MESH
F32 = jnp.float32
BF16 = jnp.bfloat16
NH = 2
PLANE = [(dy, dx) for dy in range(4) for dx in range(4) if dy or dx]
N_REMOTE = 200
STOP = None
FAR_FIRST = sorted(PLANE, key=lambda p: -min(p[0], 4 - p[0]) - min(p[1], 4 - p[1]))
VMEM_STEP = 57 << 20


def split2(v):
    hi = v.astype(BF16)
    return hi, (v - hi.astype(F32)).astype(BF16)


def split3(v):
    hi = v.astype(BF16)
    rest = v - hi.astype(F32)
    mid = rest.astype(BF16)
    return hi, mid, (rest - mid.astype(F32)).astype(BF16)


def dot(a, b):
    return jnp.dot(a, b, preferred_element_type=F32)


def column_of(row):
    n = row.shape[1]
    eye = lax.broadcasted_iota(jnp.int32, (n, n), 0) == lax.broadcasted_iota(jnp.int32, (n, n), 1)
    return jnp.sum(jnp.where(eye, jnp.broadcast_to(row, (n, n)), 0.0), axis=1, keepdims=True)


class Sent:
    def __init__(self, copy):
        self.copy, self.landed, self.left = copy, False, False

    def wait_recv(self):
        if not self.landed:
            self.copy.wait_recv()
        self.landed = True


class Loaded:
    def __init__(self, copy):
        self.copy, self.landed = copy, False

    def wait(self):
        if not self.landed:
            self.copy.wait()
        self.landed = True


def kernel(
    op_hbm, x_hbm, owner_hbm, coup_hbm, anc_hbm,
    sep_out, gath_out, coord_out,
    k32, kh, kl, xg, xl, part, core_in, zsum, z_in, at, w, f,
    ra2, ra3, rb2, rb3,
    owner_ref, anc_ref, coup_ref, loc, own, orow, gsel, outgo, coordin, top, cc, sepall,
    ss, rs, ls,
):
    row, col = lax.axis_index("row"), lax.axis_index("col")
    z, core, y, x = row // 2, row % 2, col // 4, col % 4

    def dev(dz=0, dc=0, dy=0, dx=0):
        return (((z + dz) % 4) * 2 + (core + dc) % 2, ((y + dy) % 4) * 4 + (x + dx) % 4)

    copies = []

    def send(src, dst, where):
        i = len(copies)
        c = pltpu.make_async_remote_copy(
            src_ref=src, dst_ref=dst, send_sem=ss.at[i], recv_sem=rs.at[i], device_id=where, device_id_type=MESH
        )
        c.start()
        copies.append(Sent(c))
        return copies[-1]

    xp, xm, yp, ym = dev(dx=1), dev(dx=3), dev(dy=1), dev(dy=3)
    mate = dev(dc=1)

    loads = []

    def load(src, dst):
        c = pltpu.make_async_copy(src, dst, ls.at[len(loads)])
        c.start()
        loads.append(Loaded(c))
        return loads[-1]

    x_loads = [load(x_hbm.at[pl.ds(8 * h, 8)], xg.at[h, 0, 0]) for h in range(NH)]
    k_loads = [load(op_hbm.at[pl.ds(256 * i, 256)], k32.at[pl.ds(256 * i, 256)]) for i in range(8)]
    i_loads = [load(owner_hbm, owner_ref), load(anc_hbm, anc_ref), load(coup_hbm, coup_ref)]

    barrier = pltpu.get_barrier_semaphore()
    friends = [dev(dy=dy, dx=dx) for dy, dx in PLANE] + [dev(dz=d) for d in (1, 2, 3)] + [mate]
    for d in friends:
        pl.semaphore_signal(barrier, inc=1, device_id=d, device_id_type=MESH)
    pl.semaphore_wait(barrier, len(friends))
    for c in x_loads:
        c.wait()

    A, B = pl.ds(0, 1024), pl.ds(1024, 1024)
    A0, A1, B0, B1 = pl.ds(0, 512), pl.ds(512, 512), pl.ds(1024, 512), pl.ds(1536, 512)
    ag = [dict() for _ in range(NH)]

    def own_sends(h):
        s, a = xg.at[h, 0, 0], ag[h]
        a["xp"] = send(s, xg.at[h, 0, 3], xp)
        a["xm"] = send(s, xg.at[h, 0, 1], xm)
        a["yp"] = send(s, xg.at[h, 3, 0], yp)
        a["ym"] = send(s, xg.at[h, 1, 0], ym)
        a["xo"] = send(xg.at[h, 0, 0, :, A], xg.at[h, 0, 2, :, A], dev(dx=2))
        a["yo"] = send(xg.at[h, 0, 0, :, B], xg.at[h, 2, 0, :, B], dev(dy=2))

    def to_y(h, dx):
        s = xg.at[h, 0, dx, :, A]
        return [send(s, xg.at[h, 3, dx, :, A], yp), send(s, xg.at[h, 1, dx, :, A], ym)]

    def to_x(h, dy):
        s = xg.at[h, dy, 0, :, B]
        return [send(s, xg.at[h, dy, 3, :, B], xp), send(s, xg.at[h, dy, 1, :, B], xm)]

    def step2(h):
        a = ag[h]
        a["ta"], a["tb"] = [], []
        a["xp"].wait_recv()
        a["ta"] += to_y(h, 3)
        a["yp"].wait_recv()
        a["tb"] += to_x(h, 3)
        a["xm"].wait_recv()
        a["ta"] += to_y(h, 1)
        a["ym"].wait_recv()
        a["tb"] += to_x(h, 1)

    def step3(h):
        a = ag[h]
        a["xo"].wait_recv()
        a["ta"] += to_y(h, 2)
        a["yo"].wait_recv()
        a["tb"] += to_x(h, 2)

    def step4(h):
        a = ag[h]
        for c in a["ta"]:
            c.wait_recv()
        a["end"] = [
            send(xg.at[h, 3, :, :, A0], xg.at[h, 2, :, :, A0], yp),
            send(xg.at[h, 1, :, :, A1], xg.at[h, 2, :, :, A1], ym),
        ]
        for c in a["tb"]:
            c.wait_recv()
        a["end"] += [
            send(xg.at[h, :, 3, :, B0], xg.at[h, :, 2, :, B0], xp),
            send(xg.at[h, :, 1, :, B1], xg.at[h, :, 2, :, B1], xm),
        ]

    def step5(h):
        for c in ag[h]["end"]:
            c.wait_recv()
        for q in range(8):
            rows = []
            for j in (2 * q, 2 * q + 1):
                rows.append(xg[h, (j // 4 + 4 - y) % 4, (j % 4 + 4 - x) % 4])
            hi, lo = split2(jnp.concatenate(rows, axis=0))
            xl[h, pl.ds(16 * q, 16), :] = hi
            xl[h, pl.ds(128 + 16 * q, 16), :] = lo

    def split_k(i):
        k_loads[i].wait()

        @pl.loop(0, 8)
        def _(j):
            r = pl.ds(pl.multiple_of(256 * i + 32 * j, 32), 32)
            hi, lo = split2(k32[r, :])
            kh[r, :] = hi
            kl[r, :] = lo

    def mm1(h, n):
        c = pl.ds(256 * n, 256)
        p = dot(xl[h], kh[:, c])
        p = p[:128] + p[128:] + dot(xl[h, 0:128], kl[:, c])
        part[h, :, :, :, c] = p.reshape(2, 4, 16, 256)

    ar = [dict() for _ in range(NH)]

    def ar1(h):
        ar[h]["c"] = send(part.at[h, 1 - core], core_in.at[h], mate)

    def ar2(h):
        ar[h]["c"].wait_recv()
        zsum[h] = part[h, core] + core_in[h]
        ar[h]["z"] = [send(zsum.at[h, (z + d) % 4], z_in.at[h, d - 1], dev(dz=d)) for d in (2, 1, 3)]

    def ar3(h):
        for c in ar[h]["z"]:
            c.wait_recv()
        at[h, core, z] = zsum[h, z] + z_in[h, 0] + z_in[h, 1] + z_in[h, 2]
        s = at.at[h, core, z]
        ar[h]["g"] = [(d, send(s, s, dev(dz=d))) for d in (2, 1, 3)]
        ar[h]["m"] = [send(s, s, mate)]

    def ar4(h):
        for d, c in sorted(ar[h]["g"], key=lambda t: t[0] % 2 == 0):
            c.wait_recv()
            s = at.at[h, core, (z + 4 - d) % 4]
            ar[h]["m"].append(send(s, s, mate))

    def ar5(h):
        for c in ar[h]["m"]:
            c.wait_recv()
        for n in range(8):
            c = pl.ds(128 * n, 128)
            hi, lo = split2(at[h, :, :, :, c].reshape(128, 128).T)
            w[h, c, 0:128] = hi
            w[h, c, 128:256] = lo

    def mm2(h, slots):
        for dy, dx in slots:
            b = ((y + dy) % 4) * 4 + (x + dx) % 4
            r = pl.ds(pl.multiple_of(b * 128, 128), 128)
            p = dot(kh[r, :], w[h])
            f[h, dy, dx] = p[:, :128] + p[:, 128:] + dot(kl[r, :], w[h, :, 0:128])

    rc = [dict() for _ in range(NH)]
    lo64, hi64 = pl.ds(0, 64), pl.ds(64, 64)

    def to_rows(h, dx):
        rc[h]["a2"].append(send(f.at[h, :, dx, lo64], ra2.at[h, dx - 1], dev(dx=dx)))

    def to_columns(h, dy):
        rc[h]["b2"].append(send(f.at[h, dy, :, hi64], rb2.at[h, dy - 1], dev(dy=dy)))

    def rs1(h):
        rc[h]["a2"], rc[h]["b2"] = [], []
        mm2(h, [(dy, 2) for dy in range(4)])
        to_rows(h, 2)
        mm2(h, [(2, dx) for dx in (0, 1, 3)])
        to_columns(h, 2)
        mm2(h, [(0, 1), (1, 1), (3, 1)])
        to_rows(h, 1)
        mm2(h, [(1, 0), (1, 3)])
        to_columns(h, 1)
        mm2(h, [(0, 3), (3, 3)])
        to_rows(h, 3)
        mm2(h, [(3, 0)])
        to_columns(h, 3)
        mm2(h, [(0, 0)])

    def rs3(h):
        for c in rc[h]["a2"]:
            c.wait_recv()
        f[h, :, 0, 0:64] += ra2[h, 0] + ra2[h, 1] + ra2[h, 2]
        rc[h]["a3"] = [send(f.at[h, d, 0, lo64], ra3.at[h, d - 1], dev(dy=d)) for d in (2, 1, 3)]
        for c in rc[h]["b2"]:
            c.wait_recv()
        f[h, 0, :, 64:128] += rb2[h, 0] + rb2[h, 1] + rb2[h, 2]
        rc[h]["b3"] = [send(f.at[h, 0, d, hi64], rb3.at[h, d - 1], dev(dx=d)) for d in (2, 1, 3)]

    def rs5(h):
        for c in rc[h]["b3"]:
            c.wait_recv()
        loc[h, 64:128] = f[h, 0, 0, 64:128] + rb3[h, 0] + rb3[h, 1] + rb3[h, 2]

    def rs6(h):
        for c in rc[h]["a3"]:
            c.wait_recv()
        loc[h, 0:64] = f[h, 0, 0, 0:64] + ra3[h, 0] + ra3[h, 1] + ra3[h, 2]

    def select_modes():
        for c in i_loads:
            c.wait()
        orow[...] = jnp.full((1, 128), -1.0, F32)
        orow[:, 0:88] = owner_ref[...].astype(F32)
        r = orow[...]
        c = column_of(r)
        q, p = lax.broadcasted_iota(jnp.int32, (128, 128), 0), lax.broadcasted_iota(jnp.int32, (128, 128), 1)
        rank = jnp.sum(jnp.where((c == r) & (q < p), 1.0, 0.0), axis=0, keepdims=True)
        target = jnp.where(r < 0.0, -1.0, r * 16.0 + rank)
        slot = lax.broadcasted_iota(jnp.int32, (256, 128), 0).astype(F32)
        own[...] = jnp.where(slot == target, 1.0, 0.0).astype(BF16)

    def select_ancestors():
        for i in range(4):
            c = column_of(anc_ref[:, pl.ds(128 * i, 128)].astype(F32))
            for j in range(3):
                place = lax.broadcasted_iota(jnp.int32, (128, 512), 1).astype(F32) + 512.0 * j
                gsel[pl.ds(128 * i, 128), pl.ds(512 * j, 512)] = jnp.where(c == place, 1.0, 0.0).astype(BF16)

    t = [dict() for _ in range(NH)]

    def top_z(h):
        top[h, z, core, col] = loc[h, 120:128]
        s = top.at[h, z, core, col]
        t[h]["tz"] = [send(s, s, dev(dz=d)) for d in (2, 1, 3)]

    def top_plane(h):
        for c in t[h]["tz"]:
            c.wait_recv()
        s = top.at[h, :, core, col]
        t[h]["tp"] = [send(s, s, dev(dy=dy, dx=dx)) for dy, dx in FAR_FIRST]

    def mode_send(h):
        hi, lo = split2(loc[h])
        out = dot(own[...], jnp.concatenate([hi, lo], axis=1))
        outgo[h] = (out[:, :128] + out[:, 128:]).reshape(16, 16, 128)
        coordin[h, col] = outgo[h, col]
        t[h]["mx"] = []
        for dy, dx in FAR_FIRST:
            d = dev(dy=dy, dx=dx)
            t[h]["mx"].append(send(outgo.at[h, d[1]], coordin.at[h, col], d))

    def top_core(h):
        for c in t[h]["tp"]:
            c.wait_recv()
        s = top.at[h, :, core]
        t[h]["tc"] = send(s, s, mate)

    def split_coupling():
        ch, cl = split2(coup_ref[...])
        cc[0:32, :] = ch
        cc[32:64, :] = cl

    def separators(h):
        t[h]["tc"].wait_recv()
        hi, lo = split2(top[h].reshape(1024, 128))
        c = jnp.concatenate([hi, lo], axis=1)
        p = dot(cc[...], c)
        sep = loc[h, 88:120] + (p[:32, :128] + p[:32, 128:] + p[32:, :128])
        sep_out[h] = sep
        sepall[h, col] = sep
        s = sepall.at[h, col]
        t[h]["se"] = [send(s, s, dev(dy=dy, dx=dx)) for dy, dx in FAR_FIRST]
        t[h]["cand"] = c

    def gather_top(h):
        t[h]["gath"] = dot(gsel[:, 0:1024], t[h]["cand"])

    def mode_recv(h):
        for c in t[h]["mx"]:
            c.wait_recv()
        coord_out[h] = coordin[h].reshape(256, 128)

    def gather_sep(h):
        for c in t[h]["se"]:
            c.wait_recv()
        hi, lo = split2(sepall[h].reshape(512, 128))
        gath = t[h]["gath"] + dot(gsel[:, 1024:1536], jnp.concatenate([hi, lo], axis=1))
        gath_out[h] = gath.astype(BF16)

    def settle():
        for c in copies:
            if c.landed and not c.left:
                c.copy.wait_send()
                c.left = True

    def sent():
        for c in copies:
            c.wait_recv()
        settle()
        for c in loads:
            c.wait()

    program = [
        (own_sends, 0), (own_sends, 1), (select_modes,), (select_ancestors,), (split_coupling,),
        (step2, 0), (step3, 0), (split_k, 0), (split_k, 1), (split_k, 2), (split_k, 3), (step2, 1), (step3, 1),
        (split_k, 4), (split_k, 5), (split_k, 6), (split_k, 7), (step4, 0), (step4, 1), (step5, 0),
        (mm1, 0, 0), (mm1, 0, 1), (mm1, 0, 2), (mm1, 0, 3), (ar1, 0), (ar2, 0), (step5, 1),
        (mm1, 1, 0), (mm1, 1, 1), (mm1, 1, 2), (mm1, 1, 3), (ar1, 1), (ar2, 1), (ar3, 0),
        (settle,), (ar4, 0), (ar3, 1), (ar5, 0), (rs1, 0), (ar4, 1), (ar5, 1), (rs1, 1), (settle,), (rs3, 0),
        (rs5, 0), (top_z, 0), (rs6, 0), (rs3, 1), (top_plane, 0), (mode_send, 0), (rs5, 1), (top_z, 1), (rs6, 1),
        (settle,), (top_plane, 1), (top_core, 0), (mode_send, 1), (separators, 0), (settle,), (top_core, 1), (gather_top, 0),
        (separators, 1), (gather_top, 1), (settle,), (gather_sep, 0), (mode_recv, 0), (mode_recv, 1), (settle,), (gather_sep, 1),
    ]
    for step, *args in program[:STOP] + [(sent,)]:
        step(*args)


def last(cm_ref, lm_ref, sep_ref, gath_ref, coord_ref, sep_out, int_out, gh, gl, ch, cl):
    @pl.when(pl.program_id(0) == 0)
    def _():
        pv, pp = lax.broadcasted_iota(jnp.int32, (256, 256), 1), lax.broadcasted_iota(jnp.int32, (256, 256), 0)
        order = jnp.where(pp == ((pv // 8) % 2) * 128 + (pv // 16) * 8 + pv % 8, 1.0, 0.0).astype(BF16)
        a, b, c = split3(jnp.concatenate([sep_ref[0], sep_ref[1]], axis=1))
        sep_out[...] = dot(a, order) + dot(b, order) + dot(c, order)
        gh[...] = dot(jnp.concatenate([gath_ref[0, :, 0:128], gath_ref[1, :, 0:128]], axis=1), order).astype(BF16)
        gl[...] = dot(jnp.concatenate([gath_ref[0, :, 128:256], gath_ref[1, :, 128:256]], axis=1), order).astype(BF16)
        a, b = split2(jnp.concatenate([coord_ref[0], coord_ref[1]], axis=1))
        ch[...] = dot(a, order).astype(BF16)
        cl[...] = dot(b, order).astype(BF16)

    mh, ml = split2(cm_ref[...])
    total = dot(mh, gh[...]) + dot(mh, gl[...]) + dot(ml, gh[...])
    mh, ml = split2(lm_ref[...])
    int_out[...] = total + (dot(mh, ch[...]) + dot(mh, cl[...]) + dot(ml, ch[...]))


def on_device(operator, vectors, owner_map, coupling, ancestors, leaf_modes, constraint_modes):
    vmem, anywhere = pl.BlockSpec(memory_space=pltpu.VMEM), pl.BlockSpec(memory_space=pl.ANY)
    scratch = [
        ((2048, 1024), F32), ((2048, 1024), BF16), ((2048, 1024), BF16),
        ((NH, 4, 4, 8, 2048), F32), ((NH, 256, 2048), BF16),
        ((NH, 2, 4, 16, 1024), F32), ((NH, 4, 16, 1024), F32),
        ((NH, 4, 16, 1024), F32), ((NH, 3, 16, 1024), F32), ((NH, 2, 4, 16, 1024), F32),
        ((NH, 1024, 256), BF16), ((NH, 4, 4, 128, 128), F32),
        ((NH, 3, 4, 64, 128), F32), ((NH, 3, 64, 128), F32),
        ((NH, 3, 4, 64, 128), F32), ((NH, 3, 64, 128), F32),
        ((1, 88), jnp.int32), ((1, 512), jnp.int32), ((32, 1024), F32),
        ((NH, 128, 128), F32), ((256, 128), BF16), ((1, 128), F32), ((512, 1536), BF16),
        ((NH, 16, 16, 128), F32), ((NH, 16, 16, 128), F32), ((NH, 4, 2, 16, 8, 128), F32),
        ((64, 1024), BF16), ((NH, 16, 32, 128), F32),
    ]
    sep, gath, coords = pl.pallas_call(
        kernel,
        out_shape=(
            jax.ShapeDtypeStruct((NH, 32, 128), F32),
            jax.ShapeDtypeStruct((NH, 512, 256), BF16),
            jax.ShapeDtypeStruct((NH, 256, 128), F32),
        ),
        in_specs=[anywhere] * 5,
        out_specs=(vmem, vmem, vmem),
        scratch_shapes=[pltpu.VMEM(s, t) for s, t in scratch]
        + [pltpu.SemaphoreType.DMA((N_REMOTE,)), pltpu.SemaphoreType.DMA((N_REMOTE,)), pltpu.SemaphoreType.DMA((16,))],
        compiler_params=pltpu.CompilerParams(collective_id=0, has_side_effects=True, vmem_limit_bytes=VMEM_STEP),
        cost_estimate=pl.CostEstimate(flops=9_000_000_000, bytes_accessed=20_000_000, transcendentals=0),
        name="step",
    )(operator, vectors.T, owner_map.reshape(1, 88), coupling[0], ancestors[0])

    def whole(*shape):
        return pl.BlockSpec(shape, lambda i: (0,) * len(shape))

    def rows(width):
        return pl.BlockSpec((1024, width), lambda i: (i, 0))

    separators, interiors = pl.pallas_call(
        last,
        grid=(2,),
        out_shape=(jax.ShapeDtypeStruct((32, 256), F32), jax.ShapeDtypeStruct((2048, 256), F32)),
        in_specs=[rows(512), rows(256), whole(NH, 32, 128), whole(NH, 512, 256), whole(NH, 256, 128)],
        out_specs=(whole(32, 256), rows(256)),
        scratch_shapes=[pltpu.VMEM(s, BF16) for s in ((512, 256), (512, 256), (256, 256), (256, 256))],
        compiler_params=pltpu.CompilerParams(vmem_limit_bytes=57 << 20),
        name="last",
    )(constraint_modes[0, 0], leaf_modes[0, 0], sep, gath, coords)
    return separators[None], interiors[None, None]


def solution(mesh):
    in_specs = (
        P("row", "col"),
        P("row", "col"),
        P(("row", "col"), None),
        P("row", "col", None),
        P("row", "col", None),
        P("row", "col", None, None),
        P("row", "col", None, None),
    )
    out_specs = (P("row", "col", None), P("row", "col", None, None))
    return jax.shard_map(
        on_device, mesh=mesh, in_specs=in_specs, out_specs=out_specs, check_vma=False
    )
```

```python
import functools

import jax
import jax.numpy as jnp
from jax import lax
from jax.experimental import pallas as pl
from jax.experimental.pallas import tpu as pltpu
from jax.sharding import PartitionSpec as P

MESH = pl.DeviceIdType.MESH
F32 = jnp.float32
BF16 = jnp.bfloat16
NH = 2
PLANE = [(dy, dx) for dy in range(4) for dx in range(4) if dy or dx]
N_REMOTE = 200
STOP = None
FAR_FIRST = sorted(PLANE, key=lambda p: -min(p[0], 4 - p[0]) - min(p[1], 4 - p[1]))
VMEM_STEP = 57 << 20


def split2(v):
    hi = v.astype(BF16)
    return hi, (v - hi.astype(F32)).astype(BF16)


def split3(v):
    hi = v.astype(BF16)
    rest = v - hi.astype(F32)
    mid = rest.astype(BF16)
    return hi, mid, (rest - mid.astype(F32)).astype(BF16)


def dot(a, b):
    return jnp.dot(a, b, preferred_element_type=F32)


def column_of(row):
    n = row.shape[1]
    eye = lax.broadcasted_iota(jnp.int32, (n, n), 0) == lax.broadcasted_iota(jnp.int32, (n, n), 1)
    return jnp.sum(jnp.where(eye, jnp.broadcast_to(row, (n, n)), 0.0), axis=1, keepdims=True)


class Sent:
    def __init__(self, copy):
        self.copy, self.landed, self.left = copy, False, False

    def wait_recv(self):
        if not self.landed:
            self.copy.wait_recv()
        self.landed = True


class Loaded:
    def __init__(self, copy):
        self.copy, self.landed = copy, False

    def wait(self):
        if not self.landed:
            self.copy.wait()
        self.landed = True


def kernel(
    op_hbm, x_hbm, owner_hbm, coup_hbm, anc_hbm,
    sep_out, gath_out, coord_out,
    k32, kh, kl, xg, xl, part, core_in, zsum, z_in, at, w, f,
    ra2, ra3, rb2, rb3,
    owner_ref, anc_ref, coup_ref, loc, own, orow, gsel, outgo, coordin, top, cc, sepall,
    ss, rs, ls,
):
    row, col = lax.axis_index("row"), lax.axis_index("col")
    z, core, y, x = row // 2, row % 2, col // 4, col % 4

    def dev(dz=0, dc=0, dy=0, dx=0):
        return (((z + dz) % 4) * 2 + (core + dc) % 2, ((y + dy) % 4) * 4 + (x + dx) % 4)

    copies = []

    def send(src, dst, where):
        i = len(copies)
        c = pltpu.make_async_remote_copy(
            src_ref=src, dst_ref=dst, send_sem=ss.at[i], recv_sem=rs.at[i], device_id=where, device_id_type=MESH
        )
        c.start()
        copies.append(Sent(c))
        return copies[-1]

    xp, xm, yp, ym = dev(dx=1), dev(dx=3), dev(dy=1), dev(dy=3)
    mate = dev(dc=1)

    loads = []

    def load(src, dst):
        c = pltpu.make_async_copy(src, dst, ls.at[len(loads)])
        c.start()
        loads.append(Loaded(c))
        return loads[-1]

    x_loads = [load(x_hbm.at[pl.ds(8 * h, 8)], xg.at[h, 0, 0]) for h in range(NH)]
    k_loads = [load(op_hbm.at[pl.ds(256 * i, 256)], k32.at[pl.ds(256 * i, 256)]) for i in range(8)]
    i_loads = [load(owner_hbm, owner_ref), load(anc_hbm, anc_ref), load(coup_hbm, coup_ref)]

    barrier = pltpu.get_barrier_semaphore()
    friends = [dev(dy=dy, dx=dx) for dy, dx in PLANE] + [dev(dz=d) for d in (1, 2, 3)] + [mate]
    for d in friends:
        pl.semaphore_signal(barrier, inc=1, device_id=d, device_id_type=MESH)
    pl.semaphore_wait(barrier, len(friends))
    for c in x_loads:
        c.wait()

    A, B = pl.ds(0, 1024), pl.ds(1024, 1024)
    A0, A1, B0, B1 = pl.ds(0, 512), pl.ds(512, 512), pl.ds(1024, 512), pl.ds(1536, 512)
    ag = [dict() for _ in range(NH)]

    def own_sends(h):
        s, a = xg.at[h, 0, 0], ag[h]
        a["xp"] = send(s, xg.at[h, 0, 3], xp)
        a["xm"] = send(s, xg.at[h, 0, 1], xm)
        a["yp"] = send(s, xg.at[h, 3, 0], yp)
        a["ym"] = send(s, xg.at[h, 1, 0], ym)
        a["xo"] = send(xg.at[h, 0, 0, :, A], xg.at[h, 0, 2, :, A], dev(dx=2))
        a["yo"] = send(xg.at[h, 0, 0, :, B], xg.at[h, 2, 0, :, B], dev(dy=2))

    def to_y(h, dx):
        s = xg.at[h, 0, dx, :, A]
        return [send(s, xg.at[h, 3, dx, :, A], yp), send(s, xg.at[h, 1, dx, :, A], ym)]

    def to_x(h, dy):
        s = xg.at[h, dy, 0, :, B]
        return [send(s, xg.at[h, dy, 3, :, B], xp), send(s, xg.at[h, dy, 1, :, B], xm)]

    def step2(h):
        a = ag[h]
        a["ta"], a["tb"] = [], []
        a["xp"].wait_recv()
        a["ta"] += to_y(h, 3)
        a["yp"].wait_recv()
        a["tb"] += to_x(h, 3)
        a["xm"].wait_recv()
        a["ta"] += to_y(h, 1)
        a["ym"].wait_recv()
        a["tb"] += to_x(h, 1)

    def step3(h):
        a = ag[h]
        a["xo"].wait_recv()
        a["ta"] += to_y(h, 2)
        a["yo"].wait_recv()
        a["tb"] += to_x(h, 2)

    def step4(h):
        a = ag[h]
        for c in a["ta"]:
            c.wait_recv()
        a["end"] = [
            send(xg.at[h, 3, :, :, A0], xg.at[h, 2, :, :, A0], yp),
            send(xg.at[h, 1, :, :, A1], xg.at[h, 2, :, :, A1], ym),
        ]
        for c in a["tb"]:
            c.wait_recv()
        a["end"] += [
            send(xg.at[h, :, 3, :, B0], xg.at[h, :, 2, :, B0], xp),
            send(xg.at[h, :, 1, :, B1], xg.at[h, :, 2, :, B1], xm),
        ]

    def step5(h):
        for c in ag[h]["end"]:
            c.wait_recv()
        for q in range(8):
            rows = []
            for j in (2 * q, 2 * q + 1):
                rows.append(xg[h, (j // 4 + 4 - y) % 4, (j % 4 + 4 - x) % 4])
            hi, lo = split2(jnp.concatenate(rows, axis=0))
            xl[h, pl.ds(16 * q, 16), :] = hi
            xl[h, pl.ds(128 + 16 * q, 16), :] = lo

    def split_k(i):
        k_loads[i].wait()

        @pl.loop(0, 8)
        def _(j):
            r = pl.ds(pl.multiple_of(256 * i + 32 * j, 32), 32)
            hi, lo = split2(k32[r, :])
            kh[r, :] = hi
            kl[r, :] = lo

    def mm1(h, n):
        c = pl.ds(256 * n, 256)
        p = dot(xl[h], kh[:, c])
        p = p[:128] + p[128:] + dot(xl[h, 0:128], kl[:, c])
        part[h, :, :, :, c] = p.reshape(2, 4, 16, 256)

    ar = [dict() for _ in range(NH)]

    def ar1(h):
        ar[h]["c"] = send(part.at[h, 1 - core], core_in.at[h], mate)

    def ar2(h):
        ar[h]["c"].wait_recv()
        zsum[h] = part[h, core] + core_in[h]
        ar[h]["z"] = [send(zsum.at[h, (z + d) % 4], z_in.at[h, d - 1], dev(dz=d)) for d in (2, 1, 3)]

    def ar3(h):
        for c in ar[h]["z"]:
            c.wait_recv()
        at[h, core, z] = zsum[h, z] + z_in[h, 0] + z_in[h, 1] + z_in[h, 2]
        s = at.at[h, core, z]
        ar[h]["g"] = [(d, send(s, s, dev(dz=d))) for d in (2, 1, 3)]
        ar[h]["m"] = [send(s, s, mate)]

    def ar4(h):
        for d, c in sorted(ar[h]["g"], key=lambda t: t[0] % 2 == 0):
            c.wait_recv()
            s = at.at[h, core, (z + 4 - d) % 4]
            ar[h]["m"].append(send(s, s, mate))

    def ar5(h):
        for c in ar[h]["m"]:
            c.wait_recv()
        for n in range(8):
            c = pl.ds(128 * n, 128)
            hi, lo = split2(at[h, :, :, :, c].reshape(128, 128).T)
            w[h, c, 0:128] = hi
            w[h, c, 128:256] = lo

    def mm2(h, slots):
        for dy, dx in slots:
            b = ((y + dy) % 4) * 4 + (x + dx) % 4
            r = pl.ds(pl.multiple_of(b * 128, 128), 128)
            p = dot(kh[r, :], w[h])
            f[h, dy, dx] = p[:, :128] + p[:, 128:] + dot(kl[r, :], w[h, :, 0:128])

    rc = [dict() for _ in range(NH)]
    lo64, hi64 = pl.ds(0, 64), pl.ds(64, 64)

    def to_rows(h, dx):
        rc[h]["a2"].append(send(f.at[h, :, dx, lo64], ra2.at[h, dx - 1], dev(dx=dx)))

    def to_columns(h, dy):
        rc[h]["b2"].append(send(f.at[h, dy, :, hi64], rb2.at[h, dy - 1], dev(dy=dy)))

    def rs1(h):
        rc[h]["a2"], rc[h]["b2"] = [], []
        mm2(h, [(dy, 2) for dy in range(4)])
        to_rows(h, 2)
        mm2(h, [(2, dx) for dx in (0, 1, 3)])
        to_columns(h, 2)
        mm2(h, [(0, 1), (1, 1), (3, 1)])
        to_rows(h, 1)
        mm2(h, [(1, 0), (1, 3)])
        to_columns(h, 1)
        mm2(h, [(0, 3), (3, 3)])
        to_rows(h, 3)
        mm2(h, [(3, 0)])
        to_columns(h, 3)
        mm2(h, [(0, 0)])

    def rs3(h):
        for c in rc[h]["a2"]:
            c.wait_recv()
        f[h, :, 0, 0:64] += ra2[h, 0] + ra2[h, 1] + ra2[h, 2]
        rc[h]["a3"] = [send(f.at[h, d, 0, lo64], ra3.at[h, d - 1], dev(dy=d)) for d in (2, 1, 3)]
        for c in rc[h]["b2"]:
            c.wait_recv()
        f[h, 0, :, 64:128] += rb2[h, 0] + rb2[h, 1] + rb2[h, 2]
        rc[h]["b3"] = [send(f.at[h, 0, d, hi64], rb3.at[h, d - 1], dev(dx=d)) for d in (2, 1, 3)]

    def rs5(h):
        for c in rc[h]["b3"]:
            c.wait_recv()
        loc[h, 64:128] = f[h, 0, 0, 64:128] + rb3[h, 0] + rb3[h, 1] + rb3[h, 2]

    def rs6(h):
        for c in rc[h]["a3"]:
            c.wait_recv()
        loc[h, 0:64] = f[h, 0, 0, 0:64] + ra3[h, 0] + ra3[h, 1] + ra3[h, 2]

    def select_modes():
        for c in i_loads:
            c.wait()
        orow[...] = jnp.full((1, 128), -1.0, F32)
        orow[:, 0:88] = owner_ref[...].astype(F32)
        r = orow[...]
        c = column_of(r)
        q, p = lax.broadcasted_iota(jnp.int32, (128, 128), 0), lax.broadcasted_iota(jnp.int32, (128, 128), 1)
        rank = jnp.sum(jnp.where((c == r) & (q < p), 1.0, 0.0), axis=0, keepdims=True)
        target = jnp.where(r < 0.0, -1.0, r * 16.0 + rank)
        slot = lax.broadcasted_iota(jnp.int32, (256, 128), 0).astype(F32)
        own[...] = jnp.where(slot == target, 1.0, 0.0).astype(BF16)

    def select_ancestors():
        for i in range(4):
            c = column_of(anc_ref[:, pl.ds(128 * i, 128)].astype(F32))
            for j in range(3):
                place = lax.broadcasted_iota(jnp.int32, (128, 512), 1).astype(F32) + 512.0 * j
                gsel[pl.ds(128 * i, 128), pl.ds(512 * j, 512)] = jnp.where(c == place, 1.0, 0.0).astype(BF16)

    t = [dict() for _ in range(NH)]

    def top_z(h):
        top[h, z, core, col] = loc[h, 120:128]
        s = top.at[h, z, core, col]
        t[h]["tz"] = [send(s, s, dev(dz=d)) for d in (2, 1, 3)]

    def top_plane(h):
        for c in t[h]["tz"]:
            c.wait_recv()
        s = top.at[h, :, core, col]
        t[h]["tp"] = [send(s, s, dev(dy=dy, dx=dx)) for dy, dx in FAR_FIRST]

    def mode_send(h):
        hi, lo = split2(loc[h])
        out = dot(own[...], jnp.concatenate([hi, lo], axis=1))
        outgo[h] = (out[:, :128] + out[:, 128:]).reshape(16, 16, 128)
        coordin[h, col] = outgo[h, col]
        t[h]["mx"] = []
        for dy, dx in FAR_FIRST:
            d = dev(dy=dy, dx=dx)
            t[h]["mx"].append(send(outgo.at[h, d[1]], coordin.at[h, col], d))

    def top_core(h):
        for c in t[h]["tp"]:
            c.wait_recv()
        s = top.at[h, :, core]
        t[h]["tc"] = send(s, s, mate)

    def split_coupling():
        ch, cl = split2(coup_ref[...])
        cc[0:32, :] = ch
        cc[32:64, :] = cl

    def separators(h):
        t[h]["tc"].wait_recv()
        hi, lo = split2(top[h].reshape(1024, 128))
        c = jnp.concatenate([hi, lo], axis=1)
        p = dot(cc[...], c)
        sep = loc[h, 88:120] + (p[:32, :128] + p[:32, 128:] + p[32:, :128])
        sep_out[h] = sep
        sepall[h, col] = sep
        s = sepall.at[h, col]
        t[h]["se"] = [send(s, s, dev(dy=dy, dx=dx)) for dy, dx in FAR_FIRST]
        t[h]["cand"] = c

    def gather_top(h):
        t[h]["gath"] = dot(gsel[:, 0:1024], t[h]["cand"])

    def mode_recv(h):
        for c in t[h]["mx"]:
            c.wait_recv()
        coord_out[h] = coordin[h].reshape(256, 128)

    def gather_sep(h):
        for c in t[h]["se"]:
            c.wait_recv()
        hi, lo = split2(sepall[h].reshape(512, 128))
        gath = t[h]["gath"] + dot(gsel[:, 1024:1536], jnp.concatenate([hi, lo], axis=1))
        gath_out[h] = gath.astype(BF16)

    def settle():
        for c in copies:
            if c.landed and not c.left:
                c.copy.wait_send()
                c.left = True

    def sent():
        for c in copies:
            c.wait_recv()
        settle()
        for c in loads:
            c.wait()

    program = [
        (own_sends, 0), (own_sends, 1), (select_modes,), (select_ancestors,), (split_coupling,),
        (step2, 0), (step3, 0), (split_k, 0), (split_k, 1), (split_k, 2), (split_k, 3), (step2, 1), (step3, 1),
        (split_k, 4), (split_k, 5), (split_k, 6), (split_k, 7), (step4, 0), (step4, 1), (step5, 0),
        (mm1, 0, 0), (mm1, 0, 1), (mm1, 0, 2), (mm1, 0, 3), (ar1, 0), (ar2, 0), (step5, 1),
        (mm1, 1, 0), (mm1, 1, 1), (mm1, 1, 2), (mm1, 1, 3), (ar1, 1), (ar2, 1), (ar3, 0),
        (settle,), (ar4, 0), (ar3, 1), (ar5, 0), (rs1, 0), (ar4, 1), (ar5, 1), (rs1, 1), (settle,), (rs3, 0),
        (rs5, 0), (top_z, 0), (rs6, 0), (rs3, 1), (top_plane, 0), (rs5, 1), (top_z, 1), (rs6, 1),
        (settle,), (top_plane, 1), (top_core, 0), (mode_send, 0), (mode_send, 1), (separators, 0), (settle,), (top_core, 1), (gather_top, 0),
        (separators, 1), (gather_top, 1), (settle,), (gather_sep, 0), (mode_recv, 0), (mode_recv, 1), (settle,), (gather_sep, 1),
    ]
    for step, *args in program[:STOP] + [(sent,)]:
        step(*args)


def last(cm_ref, lm_ref, sep_ref, gath_ref, coord_ref, sep_out, int_out, gh, gl, ch, cl):
    @pl.when(pl.program_id(0) == 0)
    def _():
        pv, pp = lax.broadcasted_iota(jnp.int32, (256, 256), 1), lax.broadcasted_iota(jnp.int32, (256, 256), 0)
        order = jnp.where(pp == ((pv // 8) % 2) * 128 + (pv // 16) * 8 + pv % 8, 1.0, 0.0).astype(BF16)
        a, b, c = split3(jnp.concatenate([sep_ref[0], sep_ref[1]], axis=1))
        sep_out[...] = dot(a, order) + dot(b, order) + dot(c, order)
        gh[...] = dot(jnp.concatenate([gath_ref[0, :, 0:128], gath_ref[1, :, 0:128]], axis=1), order).astype(BF16)
        gl[...] = dot(jnp.concatenate([gath_ref[0, :, 128:256], gath_ref[1, :, 128:256]], axis=1), order).astype(BF16)
        a, b = split2(jnp.concatenate([coord_ref[0], coord_ref[1]], axis=1))
        ch[...] = dot(a, order).astype(BF16)
        cl[...] = dot(b, order).astype(BF16)

    mh, ml = split2(cm_ref[...])
    total = dot(mh, gh[...]) + dot(mh, gl[...]) + dot(ml, gh[...])
    mh, ml = split2(lm_ref[...])
    int_out[...] = total + (dot(mh, ch[...]) + dot(mh, cl[...]) + dot(ml, ch[...]))


def on_device(operator, vectors, owner_map, coupling, ancestors, leaf_modes, constraint_modes):
    vmem, anywhere = pl.BlockSpec(memory_space=pltpu.VMEM), pl.BlockSpec(memory_space=pl.ANY)
    scratch = [
        ((2048, 1024), F32), ((2048, 1024), BF16), ((2048, 1024), BF16),
        ((NH, 4, 4, 8, 2048), F32), ((NH, 256, 2048), BF16),
        ((NH, 2, 4, 16, 1024), F32), ((NH, 4, 16, 1024), F32),
        ((NH, 4, 16, 1024), F32), ((NH, 3, 16, 1024), F32), ((NH, 2, 4, 16, 1024), F32),
        ((NH, 1024, 256), BF16), ((NH, 4, 4, 128, 128), F32),
        ((NH, 3, 4, 64, 128), F32), ((NH, 3, 64, 128), F32),
        ((NH, 3, 4, 64, 128), F32), ((NH, 3, 64, 128), F32),
        ((1, 88), jnp.int32), ((1, 512), jnp.int32), ((32, 1024), F32),
        ((NH, 128, 128), F32), ((256, 128), BF16), ((1, 128), F32), ((512, 1536), BF16),
        ((NH, 16, 16, 128), F32), ((NH, 16, 16, 128), F32), ((NH, 4, 2, 16, 8, 128), F32),
        ((64, 1024), BF16), ((NH, 16, 32, 128), F32),
    ]
    sep, gath, coords = pl.pallas_call(
        kernel,
        out_shape=(
            jax.ShapeDtypeStruct((NH, 32, 128), F32),
            jax.ShapeDtypeStruct((NH, 512, 256), BF16),
            jax.ShapeDtypeStruct((NH, 256, 128), F32),
        ),
        in_specs=[anywhere] * 5,
        out_specs=(vmem, vmem, vmem),
        scratch_shapes=[pltpu.VMEM(s, t) for s, t in scratch]
        + [pltpu.SemaphoreType.DMA((N_REMOTE,)), pltpu.SemaphoreType.DMA((N_REMOTE,)), pltpu.SemaphoreType.DMA((16,))],
        compiler_params=pltpu.CompilerParams(collective_id=0, has_side_effects=True, vmem_limit_bytes=VMEM_STEP),
        cost_estimate=pl.CostEstimate(flops=9_000_000_000, bytes_accessed=20_000_000, transcendentals=0),
        name="step",
    )(operator, vectors.T, owner_map.reshape(1, 88), coupling[0], ancestors[0])

    def whole(*shape):
        return pl.BlockSpec(shape, lambda i: (0,) * len(shape))

    def rows(width):
        return pl.BlockSpec((1024, width), lambda i: (i, 0))

    separators, interiors = pl.pallas_call(
        last,
        grid=(2,),
        out_shape=(jax.ShapeDtypeStruct((32, 256), F32), jax.ShapeDtypeStruct((2048, 256), F32)),
        in_specs=[rows(512), rows(256), whole(NH, 32, 128), whole(NH, 512, 256), whole(NH, 256, 128)],
        out_specs=(whole(32, 256), rows(256)),
        scratch_shapes=[pltpu.VMEM(s, BF16) for s in ((512, 256), (512, 256), (256, 256), (256, 256))],
        compiler_params=pltpu.CompilerParams(vmem_limit_bytes=57 << 20),
        name="last",
    )(constraint_modes[0, 0], leaf_modes[0, 0], sep, gath, coords)
    return separators[None], interiors[None, None]


def solution(mesh):
    in_specs = (
        P("row", "col"),
        P("row", "col"),
        P(("row", "col"), None),
        P("row", "col", None),
        P("row", "col", None),
        P("row", "col", None, None),
        P("row", "col", None, None),
    )
    out_specs = (P("row", "col", None), P("row", "col", None, None))
    return jax.shard_map(
        on_device, mesh=mesh, in_specs=in_specs, out_specs=out_specs, check_vma=False
    )
```

```python
import functools

import jax
import jax.numpy as jnp
from jax import lax
from jax.experimental import pallas as pl
from jax.experimental.pallas import tpu as pltpu
from jax.sharding import PartitionSpec as P

MESH = pl.DeviceIdType.MESH
F32 = jnp.float32
BF16 = jnp.bfloat16
NH = 2
PLANE = [(dy, dx) for dy in range(4) for dx in range(4) if dy or dx]
N_REMOTE = 200
STOP = None
FAR_FIRST = sorted(PLANE, key=lambda p: -min(p[0], 4 - p[0]) - min(p[1], 4 - p[1]))
VMEM_STEP = 57 << 20


def split2(v):
    hi = v.astype(BF16)
    return hi, (v - hi.astype(F32)).astype(BF16)


def split3(v):
    hi = v.astype(BF16)
    rest = v - hi.astype(F32)
    mid = rest.astype(BF16)
    return hi, mid, (rest - mid.astype(F32)).astype(BF16)


def dot(a, b):
    return jnp.dot(a, b, preferred_element_type=F32)


def column_of(row):
    n = row.shape[1]
    eye = lax.broadcasted_iota(jnp.int32, (n, n), 0) == lax.broadcasted_iota(jnp.int32, (n, n), 1)
    return jnp.sum(jnp.where(eye, jnp.broadcast_to(row, (n, n)), 0.0), axis=1, keepdims=True)


class Sent:
    def __init__(self, copy):
        self.copy, self.landed, self.left = copy, False, False

    def wait_recv(self):
        if not self.landed:
            self.copy.wait_recv()
        self.landed = True


class Loaded:
    def __init__(self, copy):
        self.copy, self.landed = copy, False

    def wait(self):
        if not self.landed:
            self.copy.wait()
        self.landed = True


def kernel(
    op_hbm, x_hbm, owner_hbm, coup_hbm, anc_hbm,
    sep_out, gath_out, coord_out,
    k32, kh, kl, xg, xl, part, core_in, zsum, z_in, at, w, f,
    ra2, ra3, rb2, rb3,
    owner_ref, anc_ref, coup_ref, loc, own, orow, gsel, outgo, coordin, top, cc, sepall,
    ss, rs, ls,
):
    row, col = lax.axis_index("row"), lax.axis_index("col")
    z, core, y, x = row // 2, row % 2, col // 4, col % 4

    def dev(dz=0, dc=0, dy=0, dx=0):
        return (((z + dz) % 4) * 2 + (core + dc) % 2, ((y + dy) % 4) * 4 + (x + dx) % 4)

    copies = []

    def send(src, dst, where):
        i = len(copies)
        c = pltpu.make_async_remote_copy(
            src_ref=src, dst_ref=dst, send_sem=ss.at[i], recv_sem=rs.at[i], device_id=where, device_id_type=MESH
        )
        c.start()
        copies.append(Sent(c))
        return copies[-1]

    xp, xm, yp, ym = dev(dx=1), dev(dx=3), dev(dy=1), dev(dy=3)
    mate = dev(dc=1)

    loads = []

    def load(src, dst):
        c = pltpu.make_async_copy(src, dst, ls.at[len(loads)])
        c.start()
        loads.append(Loaded(c))
        return loads[-1]

    x_loads = [load(x_hbm.at[pl.ds(8 * h, 8)], xg.at[h, 0, 0]) for h in range(NH)]
    k_loads = [load(op_hbm.at[pl.ds(256 * i, 256)], k32.at[pl.ds(256 * i, 256)]) for i in range(8)]
    i_loads = [load(owner_hbm, owner_ref), load(anc_hbm, anc_ref), load(coup_hbm, coup_ref)]

    barrier = pltpu.get_barrier_semaphore()
    friends = [dev(dy=dy, dx=dx) for dy, dx in PLANE] + [dev(dz=d) for d in (1, 2, 3)] + [mate]
    for d in friends:
        pl.semaphore_signal(barrier, inc=1, device_id=d, device_id_type=MESH)
    pl.semaphore_wait(barrier, len(friends))
    for c in x_loads:
        c.wait()

    A, B = pl.ds(0, 1024), pl.ds(1024, 1024)
    A0, A1, B0, B1 = pl.ds(0, 512), pl.ds(512, 512), pl.ds(1024, 512), pl.ds(1536, 512)
    ag = [dict() for _ in range(NH)]

    def own_sends(h):
        s, a = xg.at[h, 0, 0], ag[h]
        a["xp"] = send(s, xg.at[h, 0, 3], xp)
        a["xm"] = send(s, xg.at[h, 0, 1], xm)
        a["yp"] = send(s, xg.at[h, 3, 0], yp)
        a["ym"] = send(s, xg.at[h, 1, 0], ym)
        a["xo"] = send(xg.at[h, 0, 0, :, A], xg.at[h, 0, 2, :, A], dev(dx=2))
        a["yo"] = send(xg.at[h, 0, 0, :, B], xg.at[h, 2, 0, :, B], dev(dy=2))

    def to_y(h, dx):
        s = xg.at[h, 0, dx, :, A]
        return [send(s, xg.at[h, 3, dx, :, A], yp), send(s, xg.at[h, 1, dx, :, A], ym)]

    def to_x(h, dy):
        s = xg.at[h, dy, 0, :, B]
        return [send(s, xg.at[h, dy, 3, :, B], xp), send(s, xg.at[h, dy, 1, :, B], xm)]

    def step2(h):
        a = ag[h]
        a["ta"], a["tb"] = [], []
        a["xp"].wait_recv()
        a["ta"] += to_y(h, 3)
        a["yp"].wait_recv()
        a["tb"] += to_x(h, 3)
        a["xm"].wait_recv()
        a["ta"] += to_y(h, 1)
        a["ym"].wait_recv()
        a["tb"] += to_x(h, 1)

    def step3(h):
        a = ag[h]
        a["xo"].wait_recv()
        a["ta"] += to_y(h, 2)
        a["yo"].wait_recv()
        a["tb"] += to_x(h, 2)

    def step4(h):
        a = ag[h]
        for c in a["ta"]:
            c.wait_recv()
        a["end"] = [
            send(xg.at[h, 3, :, :, A0], xg.at[h, 2, :, :, A0], yp),
            send(xg.at[h, 1, :, :, A1], xg.at[h, 2, :, :, A1], ym),
        ]
        for c in a["tb"]:
            c.wait_recv()
        a["end"] += [
            send(xg.at[h, :, 3, :, B0], xg.at[h, :, 2, :, B0], xp),
            send(xg.at[h, :, 1, :, B1], xg.at[h, :, 2, :, B1], xm),
        ]

    def step5(h):
        for c in ag[h]["end"]:
            c.wait_recv()
        for q in range(8):
            rows = []
            for j in (2 * q, 2 * q + 1):
                rows.append(xg[h, (j // 4 + 4 - y) % 4, (j % 4 + 4 - x) % 4])
            hi, lo = split2(jnp.concatenate(rows, axis=0))
            xl[h, pl.ds(16 * q, 16), :] = hi
            xl[h, pl.ds(128 + 16 * q, 16), :] = lo

    def split_k(i):
        k_loads[i].wait()

        @pl.loop(0, 8)
        def _(j):
            r = pl.ds(pl.multiple_of(256 * i + 32 * j, 32), 32)
            hi, lo = split2(k32[r, :])
            kh[r, :] = hi
            kl[r, :] = lo

    def mm1(h, n):
        c = pl.ds(256 * n, 256)
        p = dot(xl[h], kh[:, c])
        p = p[:128] + p[128:] + dot(xl[h, 0:128], kl[:, c])
        part[h, :, :, :, c] = p.reshape(2, 4, 16, 256)

    ar = [dict() for _ in range(NH)]

    def ar1(h):
        ar[h]["c"] = send(part.at[h, 1 - core], core_in.at[h], mate)

    def ar2(h):
        ar[h]["c"].wait_recv()
        zsum[h] = part[h, core] + core_in[h]
        ar[h]["z"] = [send(zsum.at[h, (z + d) % 4], z_in.at[h, d - 1], dev(dz=d)) for d in (2, 1, 3)]

    def ar3(h):
        for c in ar[h]["z"]:
            c.wait_recv()
        at[h, core, z] = zsum[h, z] + z_in[h, 0] + z_in[h, 1] + z_in[h, 2]
        s = at.at[h, core, z]
        ar[h]["g"] = [(d, send(s, s, dev(dz=d))) for d in (2, 1, 3)]
        ar[h]["m"] = [send(s, s, mate)]

    def ar4(h):
        for d, c in sorted(ar[h]["g"], key=lambda t: t[0] % 2 == 0):
            c.wait_recv()
            s = at.at[h, core, (z + 4 - d) % 4]
            ar[h]["m"].append(send(s, s, mate))

    def ar5(h):
        for c in ar[h]["m"]:
            c.wait_recv()
        for n in range(8):
            c = pl.ds(128 * n, 128)
            hi, lo = split2(at[h, :, :, :, c].reshape(128, 128).T)
            w[h, c, 0:128] = hi
            w[h, c, 128:256] = lo

    def mm2(h, slots):
        for dy, dx in slots:
            b = ((y + dy) % 4) * 4 + (x + dx) % 4
            r = pl.ds(pl.multiple_of(b * 128, 128), 128)
            p = dot(kh[r, :], w[h])
            f[h, dy, dx] = p[:, :128] + p[:, 128:] + dot(kl[r, :], w[h, :, 0:128])

    rc = [dict() for _ in range(NH)]
    lo64, hi64 = pl.ds(0, 64), pl.ds(64, 64)

    def to_rows(h, dx):
        rc[h]["a2"].append(send(f.at[h, :, dx, lo64], ra2.at[h, dx - 1], dev(dx=dx)))

    def to_columns(h, dy):
        rc[h]["b2"].append(send(f.at[h, dy, :, hi64], rb2.at[h, dy - 1], dev(dy=dy)))

    def rs1(h):
        rc[h]["a2"], rc[h]["b2"] = [], []
        mm2(h, [(dy, 2) for dy in range(4)])
        to_rows(h, 2)
        mm2(h, [(2, dx) for dx in (0, 1, 3)])
        to_columns(h, 2)
        mm2(h, [(0, 1), (1, 1), (3, 1)])
        to_rows(h, 1)
        mm2(h, [(1, 0), (1, 3)])
        to_columns(h, 1)
        mm2(h, [(0, 3), (3, 3)])
        to_rows(h, 3)
        mm2(h, [(3, 0)])
        to_columns(h, 3)
        mm2(h, [(0, 0)])

    def rs3(h):
        for c in rc[h]["a2"]:
            c.wait_recv()
        f[h, :, 0, 0:64] += ra2[h, 0] + ra2[h, 1] + ra2[h, 2]
        rc[h]["a3"] = [send(f.at[h, d, 0, lo64], ra3.at[h, d - 1], dev(dy=d)) for d in (2, 1, 3)]
        for c in rc[h]["b2"]:
            c.wait_recv()
        f[h, 0, :, 64:128] += rb2[h, 0] + rb2[h, 1] + rb2[h, 2]
        rc[h]["b3"] = [send(f.at[h, 0, d, hi64], rb3.at[h, d - 1], dev(dx=d)) for d in (2, 1, 3)]

    def rs5(h):
        for c in rc[h]["b3"]:
            c.wait_recv()
        loc[h, 64:128] = f[h, 0, 0, 64:128] + rb3[h, 0] + rb3[h, 1] + rb3[h, 2]

    def rs6(h):
        for c in rc[h]["a3"]:
            c.wait_recv()
        loc[h, 0:64] = f[h, 0, 0, 0:64] + ra3[h, 0] + ra3[h, 1] + ra3[h, 2]

    def select_modes():
        for c in i_loads:
            c.wait()
        orow[...] = jnp.full((1, 128), -1.0, F32)
        orow[:, 0:88] = owner_ref[...].astype(F32)
        r = orow[...]
        c = column_of(r)
        q, p = lax.broadcasted_iota(jnp.int32, (128, 128), 0), lax.broadcasted_iota(jnp.int32, (128, 128), 1)
        rank = jnp.sum(jnp.where((c == r) & (q < p), 1.0, 0.0), axis=0, keepdims=True)
        target = jnp.where(r < 0.0, -1.0, r * 16.0 + rank)
        slot = lax.broadcasted_iota(jnp.int32, (256, 128), 0).astype(F32)
        own[...] = jnp.where(slot == target, 1.0, 0.0).astype(BF16)

    def select_ancestors():
        for i in range(4):
            c = column_of(anc_ref[:, pl.ds(128 * i, 128)].astype(F32))
            for j in range(3):
                place = lax.broadcasted_iota(jnp.int32, (128, 512), 1).astype(F32) + 512.0 * j
                gsel[pl.ds(128 * i, 128), pl.ds(512 * j, 512)] = jnp.where(c == place, 1.0, 0.0).astype(BF16)

    t = [dict() for _ in range(NH)]

    def top_z(h):
        top[h, z, core, col] = loc[h, 120:128]
        s = top.at[h, z, core, col]
        t[h]["tz"] = [send(s, s, dev(dz=d)) for d in (2, 1, 3)]

    def top_plane(h):
        for c in t[h]["tz"]:
            c.wait_recv()
        s = top.at[h, :, core, col]
        t[h]["tp"] = [send(s, s, dev(dy=dy, dx=dx)) for dy, dx in FAR_FIRST]

    def mode_send(h):
        hi, lo = split2(loc[h])
        out = dot(own[...], jnp.concatenate([hi, lo], axis=1))
        outgo[h] = (out[:, :128] + out[:, 128:]).reshape(16, 16, 128)
        coordin[h, col] = outgo[h, col]
        t[h]["mx"] = []
        for dy, dx in FAR_FIRST:
            d = dev(dy=dy, dx=dx)
            t[h]["mx"].append(send(outgo.at[h, d[1]], coordin.at[h, col], d))

    def top_core(h):
        for c in t[h]["tp"]:
            c.wait_recv()
        s = top.at[h, :, core]
        t[h]["tc"] = send(s, s, mate)

    def split_coupling():
        ch, cl = split2(coup_ref[...])
        cc[0:32, :] = ch
        cc[32:64, :] = cl

    def separators(h):
        t[h]["tc"].wait_recv()
        hi, lo = split2(top[h].reshape(1024, 128))
        c = jnp.concatenate([hi, lo], axis=1)
        p = dot(cc[...], c)
        sep = loc[h, 88:120] + (p[:32, :128] + p[:32, 128:] + p[32:, :128])
        sep_out[h] = sep
        sepall[h, col] = sep
        s = sepall.at[h, col]
        t[h]["se"] = [send(s, s, dev(dy=dy, dx=dx)) for dy, dx in FAR_FIRST]
        t[h]["cand"] = c

    def gather_top(h):
        t[h]["gath"] = dot(gsel[:, 0:1024], t[h]["cand"])

    def mode_recv(h):
        for c in t[h]["mx"]:
            c.wait_recv()
        coord_out[h] = coordin[h].reshape(256, 128)

    def gather_sep(h):
        for c in t[h]["se"]:
            c.wait_recv()
        hi, lo = split2(sepall[h].reshape(512, 128))
        gath = t[h]["gath"] + dot(gsel[:, 1024:1536], jnp.concatenate([hi, lo], axis=1))
        gath_out[h] = gath.astype(BF16)

    def settle():
        for c in copies:
            if c.landed and not c.left:
                c.copy.wait_send()
                c.left = True

    def sent():
        for c in copies:
            c.wait_recv()
        settle()
        for c in loads:
            c.wait()

    program = [
        (own_sends, 0), (select_modes,), (select_ancestors,), (split_coupling,),
        (step2, 0), (own_sends, 1), (step3, 0), (split_k, 0), (split_k, 1), (split_k, 2), (split_k, 3), (step2, 1), (step3, 1),
        (split_k, 4), (split_k, 5), (split_k, 6), (split_k, 7), (step4, 0), (step4, 1), (step5, 0),
        (mm1, 0, 0), (mm1, 0, 1), (mm1, 0, 2), (mm1, 0, 3), (ar1, 0), (ar2, 0), (step5, 1),
        (mm1, 1, 0), (mm1, 1, 1), (mm1, 1, 2), (mm1, 1, 3), (ar1, 1), (ar2, 1), (ar3, 0),
        (settle,), (ar4, 0), (ar3, 1), (ar5, 0), (rs1, 0), (ar4, 1), (ar5, 1), (rs1, 1), (settle,), (rs3, 0),
        (rs5, 0), (top_z, 0), (rs6, 0), (rs3, 1), (top_plane, 0), (mode_send, 0), (rs5, 1), (top_z, 1), (rs6, 1),
        (settle,), (top_plane, 1), (top_core, 0), (mode_send, 1), (separators, 0), (settle,), (top_core, 1), (gather_top, 0),
        (separators, 1), (gather_top, 1), (settle,), (gather_sep, 0), (mode_recv, 0), (mode_recv, 1), (settle,), (gather_sep, 1),
    ]
    for step, *args in program[:STOP] + [(sent,)]:
        step(*args)


def last(cm_ref, lm_ref, sep_ref, gath_ref, coord_ref, sep_out, int_out, gh, gl, ch, cl):
    @pl.when(pl.program_id(0) == 0)
    def _():
        pv, pp = lax.broadcasted_iota(jnp.int32, (256, 256), 1), lax.broadcasted_iota(jnp.int32, (256, 256), 0)
        order = jnp.where(pp == ((pv // 8) % 2) * 128 + (pv // 16) * 8 + pv % 8, 1.0, 0.0).astype(BF16)
        a, b, c = split3(jnp.concatenate([sep_ref[0], sep_ref[1]], axis=1))
        sep_out[...] = dot(a, order) + dot(b, order) + dot(c, order)
        gh[...] = dot(jnp.concatenate([gath_ref[0, :, 0:128], gath_ref[1, :, 0:128]], axis=1), order).astype(BF16)
        gl[...] = dot(jnp.concatenate([gath_ref[0, :, 128:256], gath_ref[1, :, 128:256]], axis=1), order).astype(BF16)
        a, b = split2(jnp.concatenate([coord_ref[0], coord_ref[1]], axis=1))
        ch[...] = dot(a, order).astype(BF16)
        cl[...] = dot(b, order).astype(BF16)

    mh, ml = split2(cm_ref[...])
    total = dot(mh, gh[...]) + dot(mh, gl[...]) + dot(ml, gh[...])
    mh, ml = split2(lm_ref[...])
    int_out[...] = total + (dot(mh, ch[...]) + dot(mh, cl[...]) + dot(ml, ch[...]))


def on_device(operator, vectors, owner_map, coupling, ancestors, leaf_modes, constraint_modes):
    vmem, anywhere = pl.BlockSpec(memory_space=pltpu.VMEM), pl.BlockSpec(memory_space=pl.ANY)
    scratch = [
        ((2048, 1024), F32), ((2048, 1024), BF16), ((2048, 1024), BF16),
        ((NH, 4, 4, 8, 2048), F32), ((NH, 256, 2048), BF16),
        ((NH, 2, 4, 16, 1024), F32), ((NH, 4, 16, 1024), F32),
        ((NH, 4, 16, 1024), F32), ((NH, 3, 16, 1024), F32), ((NH, 2, 4, 16, 1024), F32),
        ((NH, 1024, 256), BF16), ((NH, 4, 4, 128, 128), F32),
        ((NH, 3, 4, 64, 128), F32), ((NH, 3, 64, 128), F32),
        ((NH, 3, 4, 64, 128), F32), ((NH, 3, 64, 128), F32),
        ((1, 88), jnp.int32), ((1, 512), jnp.int32), ((32, 1024), F32),
        ((NH, 128, 128), F32), ((256, 128), BF16), ((1, 128), F32), ((512, 1536), BF16),
        ((NH, 16, 16, 128), F32), ((NH, 16, 16, 128), F32), ((NH, 4, 2, 16, 8, 128), F32),
        ((64, 1024), BF16), ((NH, 16, 32, 128), F32),
    ]
    sep, gath, coords = pl.pallas_call(
        kernel,
        out_shape=(
            jax.ShapeDtypeStruct((NH, 32, 128), F32),
            jax.ShapeDtypeStruct((NH, 512, 256), BF16),
            jax.ShapeDtypeStruct((NH, 256, 128), F32),
        ),
        in_specs=[anywhere] * 5,
        out_specs=(vmem, vmem, vmem),
        scratch_shapes=[pltpu.VMEM(s, t) for s, t in scratch]
        + [pltpu.SemaphoreType.DMA((N_REMOTE,)), pltpu.SemaphoreType.DMA((N_REMOTE,)), pltpu.SemaphoreType.DMA((16,))],
        compiler_params=pltpu.CompilerParams(collective_id=0, has_side_effects=True, vmem_limit_bytes=VMEM_STEP),
        cost_estimate=pl.CostEstimate(flops=9_000_000_000, bytes_accessed=20_000_000, transcendentals=0),
        name="step",
    )(operator, vectors.T, owner_map.reshape(1, 88), coupling[0], ancestors[0])

    def whole(*shape):
        return pl.BlockSpec(shape, lambda i: (0,) * len(shape))

    def rows(width):
        return pl.BlockSpec((1024, width), lambda i: (i, 0))

    separators, interiors = pl.pallas_call(
        last,
        grid=(2,),
        out_shape=(jax.ShapeDtypeStruct((32, 256), F32), jax.ShapeDtypeStruct((2048, 256), F32)),
        in_specs=[rows(512), rows(256), whole(NH, 32, 128), whole(NH, 512, 256), whole(NH, 256, 128)],
        out_specs=(whole(32, 256), rows(256)),
        scratch_shapes=[pltpu.VMEM(s, BF16) for s in ((512, 256), (512, 256), (256, 256), (256, 256))],
        compiler_params=pltpu.CompilerParams(vmem_limit_bytes=57 << 20),
        name="last",
    )(constraint_modes[0, 0], leaf_modes[0, 0], sep, gath, coords)
    return separators[None], interiors[None, None]


def solution(mesh):
    in_specs = (
        P("row", "col"),
        P("row", "col"),
        P(("row", "col"), None),
        P("row", "col", None),
        P("row", "col", None),
        P("row", "col", None, None),
        P("row", "col", None, None),
    )
    out_specs = (P("row", "col", None), P("row", "col", None, None))
    return jax.shard_map(
        on_device, mesh=mesh, in_specs=in_specs, out_specs=out_specs, check_vma=False
    )
```
